128 devices in a mesh: shell: 4 (over z_lo, core), blk: 32 (over y, z_hi, x).
Axes of the slice: x: 4, y: 4, z: 4 (z_hi: 2, z_lo: 2; z = z_hi * 2 + z_lo), core: 2. Of those that a mesh axis runs over, the one named last changes fastest.
Arguments:
- plasma_state: float32 [8, 16384, 512], P(None, ('shell', 'blk')), may hold values from -6 to 6
- jacobian: float32 [3, 8, 8, 16384], P(None, None, None, ('shell', 'blk'))
- send_list: int32 [4, 286720], P(None, ('shell', 'blk')), may hold values from 0 to 127, as said below
- recv_map: int32 [262144], P(('shell', 'blk')), may hold values from 0 to 2240, as said below
- visit_point: int32 [524288], P(('shell', 'blk')), may hold values from 0 to 131072, as said below
- visit_cell: int32 [524288], P(('shell', 'blk')), may hold values from 0 to 65535, as said below
- conductance: float32 [1024, 512], P('shell'), may hold values from 1 to 1000
- lengths: int32 [1024], P('shell'), may hold values from 128 to 500, as said below
Outputs:
- new_state: float32 [8, 16384, 512], P(None, ('shell', 'blk'))
- thread_temp: float32 [1024, 512], P(('shell', 'blk'))
The draws below stay inside these ranges and needn't reach their ends.
Inputs may be any that keep to these rules, and one draw needn't show every extreme that they name: `send_list`: row 0 is a source block of the sending device, row 1 the face opposite the receiving face, row 2 the level code (3: empty slot), row 3 the quadrant. Column s * 70 + c is slot c of what goes to the device of blk index s; some device fills all 70 slots to one peer in every draw. Level 0 stands only in slots c < 17; slots from 17 on hold levels 1, 2 or 3. `recv_map`: four entries per block and angular face, block-major then face. Each face takes one piece of level 0 or 1, or four pieces of level 2 with quadrants 0 to 3; exactly 128 faces of each device take four. Every used send slot is named exactly once. `visit_point`: t * 512 + i names point i of thread t of the device's shell group; the value 256 * 512 marks an unused slot. In a shell group every point below its thread's length is named exactly once, no other point is named. A device's slots form 8 aligned runs of 512 slots; the points named in one run belong to threads of one device (thread t to blk index t div 8), and the runs of one device name points of different devices. `visit_cell`: distinct cells of the device, block * 8^3 + cell. `lengths`: some thread of each shell group has 500 points.
All inputs are finite; a program needn't handle non-finite values. Where the reference program divides by a largest or mean magnitude, that divisor is 1e-20 or more.
Results may differ from the reference program's by a relative error of at most 0.0003.
Values sent between devices are 32-bit elements; how exact they have to be, the bound alone decides.
A program may use at most 192 MiB of HBM per device.

```python
import math
import jax
import jax.numpy as jnp
from jax import lax

NF = 8
BS = 8
BLK_DEV = 128
THR_DEV = 8
PTS = 512
MAXLEN = 500
BLOCKS = 16384
THREADS = 1024
THR_GROUP = 256
CAP = 70
FULL_SLOTS = 17
PIECES = 2240
N_SHELL = 4
N_BLK = 32
DEVICES = 128


def face_tables(key):
    faces = 4 * BLK_DEV
    entries = 7 * BLK_DEV
    first_half = entries // 2
    near_peers = N_BLK // 4
    subkeys = jax.random.split(jax.random.fold_in(key, 11), 6)
    fine_rank = jax.vmap(lambda subkey: jax.random.permutation(subkey, faces))(jax.random.split(subkeys[0], DEVICES))
    is_fine = fine_rank < BLK_DEV
    multiplicity = jnp.where(is_fine, 4, 1).astype(jnp.int32)
    starts = jnp.cumsum(multiplicity, axis=1) - multiplicity
    shuffle = jax.vmap(lambda subkey: jax.random.permutation(subkey, entries))(jax.random.split(subkeys[1], DEVICES))
    rotation = jax.random.randint(subkeys[2], (DEVICES,), 0, N_BLK)
    coarse_quad = jax.random.randint(subkeys[4], (DEVICES, faces), 0, 4)
    source_block = jax.random.randint(subkeys[5], (DEVICES, faces, 4), 0, BLK_DEV)
    slot_k = jnp.arange(4, dtype=jnp.int32)[None, None, :]
    valid = slot_k < multiplicity[:, :, None]
    entry_index = jnp.minimum(starts[:, :, None] + slot_k, entries - 1)
    position = jnp.take_along_axis(shuffle, entry_index.reshape(DEVICES, -1), axis=1).reshape(DEVICES, faces, 4)
    later_pos = position - first_half
    in_first = position < first_half
    offset = jnp.where(in_first, position % near_peers, later_pos % N_BLK)
    first_count = jnp.where(offset < near_peers, (first_half - offset + near_peers - 1) // near_peers, 0)
    slot_index = jnp.where(in_first, position // near_peers, first_count + later_pos // N_BLK)
    receiver_dev = jnp.arange(DEVICES, dtype=jnp.int32)[:, None, None]
    group_index = receiver_dev // N_BLK
    receiver = receiver_dev % N_BLK
    sender = (receiver + offset + rotation[:, None, None]) % N_BLK
    column = (group_index * N_BLK + sender) * (N_BLK * CAP) + receiver * CAP + slot_index
    shape_all = (DEVICES, faces, 4)
    coarse_level = jnp.where(slot_index[:, :, 0] < FULL_SLOTS, 0, 1).astype(jnp.int32)
    dest_face = jnp.broadcast_to(jnp.arange(faces, dtype=jnp.int32)[None, :, None] % 4, shape_all)
    level_code = jnp.broadcast_to(jnp.where(is_fine[:, :, None], 2, coarse_level[:, :, None]), shape_all)
    quadrant = jnp.where(jnp.broadcast_to(is_fine[:, :, None], shape_all), jnp.broadcast_to(slot_k, shape_all), jnp.where(level_code == 1, jnp.broadcast_to(coarse_quad[:, :, None], shape_all), 0))
    total_cols = DEVICES * N_BLK * CAP
    target = jnp.where(valid, column, total_cols).reshape(-1)
    values = jnp.stack([source_block, jnp.bitwise_xor(dest_face, 1), level_code, quadrant]).reshape(4, -1).astype(jnp.int32)
    send_table = jnp.zeros((4, total_cols), jnp.int32).at[2].set(3)
    send_table = send_table.at[:, target].set(values, mode='drop')
    recv_table = jnp.where(valid, sender * CAP + slot_index, N_BLK * CAP).reshape(-1).astype(jnp.int32)
    return (send_table, recv_table)


def thread_lengths(key):
    subkeys = jax.random.split(jax.random.fold_in(key, 21), 2)
    raw_lengths = jax.random.randint(subkeys[0], (THREADS,), PTS // 4, MAXLEN + 1)
    groups = THREADS // THR_GROUP
    longest = jax.random.randint(subkeys[1], (groups,), 0, THR_GROUP)
    thread = jnp.arange(THREADS, dtype=jnp.int32)
    is_longest = thread % THR_GROUP == longest[thread // THR_GROUP]
    return jnp.where(is_longest, MAXLEN, raw_lengths).astype(jnp.int32)


def thread_points(key):
    lengths = thread_lengths(key)
    segment = PTS // 8
    groups = THREADS // THR_GROUP
    perm_keys = jax.random.split(jax.random.fold_in(key, 22), 2)
    outer_perm = jax.vmap(lambda subkey: jax.random.permutation(subkey, N_BLK))(jax.random.split(perm_keys[0], groups))
    inner_perm = jax.vmap(lambda subkey: jax.random.permutation(subkey, N_BLK))(jax.random.split(perm_keys[1], groups))
    thread = jnp.arange(THREADS, dtype=jnp.int32)[:, None, None]
    piece_k = jnp.arange(8, dtype=jnp.int32)[None, :, None]
    within = jnp.arange(segment, dtype=jnp.int32)[None, None, :]
    group_index = thread // THR_GROUP
    local_thread = thread % THR_GROUP
    owner_dev = local_thread // THR_DEV
    dest_dev = outer_perm[group_index, (inner_perm[group_index, owner_dev] + piece_k) % N_BLK]
    slot_index = piece_k * (THR_DEV * segment) + local_thread % THR_DEV * segment + within
    point_index = piece_k * segment + within
    point_value = jnp.where(point_index < lengths[:, None, None], local_thread * PTS + point_index, THR_GROUP * PTS)
    flat_index = (group_index * N_BLK + dest_dev) * (THR_DEV * PTS) + slot_index
    shape_all = (THREADS, 8, segment)
    visits = jnp.zeros((DEVICES * THR_DEV * PTS,), jnp.int32)
    return visits.at[jnp.broadcast_to(flat_index, shape_all).reshape(-1)].set(jnp.broadcast_to(point_value, shape_all).reshape(-1).astype(jnp.int32))


def draw_send_list(key, part):
    return face_tables(key)[0]


def draw_recv_map(key, part):
    return face_tables(key)[1]


def draw_lengths(key, part):
    return thread_lengths(key)


def draw_visit_point(key, part):
    return thread_points(key)


def draw_visit_cell(key, part):
    key = jax.random.fold_in(key, 23)
    cells_dev = BLK_DEV * BS * BS * BS
    chosen = jax.vmap(lambda subkey: jax.random.permutation(subkey, cells_dev)[:THR_DEV * PTS])(jax.random.split(key, DEVICES))
    return chosen.reshape(-1).astype(jnp.int32)


def draw_jacobian(key, part):
    key = jax.random.fold_in(key, 7)
    subkeys = jax.random.split(key, 2)
    position = jnp.arange(BLOCKS, dtype=jnp.float32) / max(BLOCKS - 1, 1)
    entries_raw = jax.random.normal(subkeys[0], (3, NF, NF, BLOCKS), jnp.float32)
    rise_factor = 1.0 + 2.0 * position
    jitter = jax.random.uniform(subkeys[1], (1, 1, 1, BLOCKS), jnp.float32, 0.7, 1.3)
    return (entries_raw * (rise_factor * jitter / math.sqrt(NF))).astype(jnp.float32)


def block_scale(own_key, shape, cuts, least, largest):
    factor_of, own = 1.0, jax.random.fold_in(own_key, 6)
    for dim, blocks in cuts:
        steps = jnp.exp(jax.random.uniform(jax.random.fold_in(own, dim), (blocks,), jnp.float32, least / len(cuts), largest / len(cuts)))
        factor_of = factor_of * jnp.repeat(steps, shape[dim] // blocks).reshape([-1 if axis == dim else 1 for axis in range(len(shape))])
    return factor_of


def bell_draw(stream_key, dims, width, most, shards=(), kind=jnp.bfloat16):
    gain = block_scale(stream_key, dims, shards, -0.22, 0.18) if shards else 1.0
    values = jax.random.normal(stream_key, dims, jnp.float32) * width * gain
    return jnp.minimum(jnp.maximum(values, -most), most).astype(kind)


def setup_inputs(seed: int = 0) -> dict:
    streams_of = jax.random.split(jax.random.key(seed), 9)
    plasma_state = bell_draw(streams_of[0], (NF, BLOCKS, BS * BS * BS), 1.0, 6.0, ((1, 128),), jnp.float32)
    jacobian = draw_jacobian(jax.random.fold_in(streams_of[8], 71), 0)
    send_list = draw_send_list(jax.random.fold_in(streams_of[8], 71), 0)
    recv_map = draw_recv_map(jax.random.fold_in(streams_of[8], 71), 0)
    visit_point = draw_visit_point(jax.random.fold_in(streams_of[8], 71), 0)
    visit_cell = draw_visit_cell(jax.random.fold_in(streams_of[8], 71), 0)
    conductance = jnp.clip(jnp.exp(math.log(1000.0) - 6.9077553 * jax.random.uniform(streams_of[6], (THREADS, PTS), jnp.float32) ** block_scale(streams_of[6], (THREADS, PTS), ((0, 4),), -0.2, 0.2)), 1.0, 1000.0)
    lengths = draw_lengths(jax.random.fold_in(streams_of[8], 71), 0)
    return {"plasma_state": plasma_state, "jacobian": jacobian, "send_list": send_list, "recv_map": recv_map, "visit_point": visit_point, "visit_cell": visit_cell, "conductance": conductance, "lengths": lengths}


CFL_NUMBER = 0.3

def face_layers(plasma_state):
    fields, blocks = (plasma_state.shape[0], plasma_state.shape[1])
    cube_view = plasma_state.reshape(fields, blocks, BS, BS, BS)
    layers = jnp.stack([cube_view[:, :, :, 0, :], cube_view[:, :, :, BS - 1, :], cube_view[:, :, :, :, 0], cube_view[:, :, :, :, BS - 1]], axis=0)
    return jnp.transpose(layers, (2, 0, 1, 3, 4)).reshape(blocks * 4, fields, BS, BS)

def pack_pieces(plasma_state, send_list):
    fields = plasma_state.shape[0]
    layers = face_layers(plasma_state)
    source_row = send_list[0] * 4 + send_list[1]
    level_code = send_list[2]
    quadrant = send_list[3]
    half_edge = BS // 2
    face_rows = layers[source_row]
    quad_ids = jnp.arange(2, dtype=jnp.int32)
    quad_pick = (quadrant[:, None, None] == quad_ids[None, :, None] * 2 + quad_ids[None, None, :]).astype(jnp.float32)
    quarters = face_rows.reshape(-1, fields, 2, half_edge, 2, half_edge)
    chosen = jnp.sum(quad_pick[:, None, :, None, :, None] * quarters, axis=(2, 4))
    prolonged = jnp.repeat(jnp.repeat(chosen, 2, axis=2), 2, axis=3)
    restricted = jnp.mean(face_rows.reshape(-1, fields, half_edge, 2, half_edge, 2), axis=(3, 5))
    quad_mask = jnp.repeat(jnp.repeat(quad_pick, half_edge, axis=1), half_edge, axis=2)
    placed_rest = jnp.tile(restricted, (1, 1, 2, 2)) * quad_mask[:, None]
    level_wide = level_code[:, None, None, None]
    pieces = jnp.where(level_wide == 0, face_rows, jnp.where(level_wide == 1, prolonged, jnp.where(level_wide == 2, placed_rest, jnp.zeros_like(face_rows))))
    return pieces.reshape(pieces.shape[0], fields * BS * BS)

def assemble_ghosts(received, recv_map, blocks, fields):
    padded_rows = jnp.concatenate([received, jnp.zeros((1, received.shape[1]), jnp.float32)], axis=0)
    taken = padded_rows[recv_map].reshape(blocks, 4, 4, fields, BS, BS)
    return jnp.sum(taken, axis=2)

def face_flux(padded, matrix, wave_speed, along):
    extent = padded.shape[along]
    lower_side = lax.slice_in_dim(padded, 0, extent - 1, axis=along)
    upper_side = lax.slice_in_dim(padded, 1, extent, axis=along)
    averaged = jnp.einsum('ghb,hbxyz->gbxyz', matrix, lower_side + upper_side, precision=lax.Precision.HIGHEST)
    return 0.5 * averaged - 0.5 * wave_speed[None, :, None, None, None] * (upper_side - lower_side)

def advance(plasma_state, ghosts, lower_rim, upper_rim, jacobian, wave_speed, step_ratio):
    fields, blocks = (plasma_state.shape[0], plasma_state.shape[1])
    cube_view = plasma_state.reshape(fields, blocks, BS, BS, BS)
    ghost_fields = jnp.transpose(ghosts, (2, 0, 1, 3, 4))
    padded_radial = jnp.concatenate([lower_rim[:, :, None], cube_view, upper_rim[:, :, None]], axis=2)
    padded_first = jnp.concatenate([ghost_fields[:, :, 0][:, :, :, None], cube_view, ghost_fields[:, :, 1][:, :, :, None]], axis=3)
    padded_second = jnp.concatenate([ghost_fields[:, :, 2][..., None], cube_view, ghost_fields[:, :, 3][..., None]], axis=4)
    change_sum = jnp.zeros_like(cube_view)
    for direction, padded in enumerate((padded_radial, padded_first, padded_second)):
        along = direction + 2
        face_values = face_flux(padded, jacobian[direction], wave_speed[direction], along)
        extent = face_values.shape[along]
        change_sum = change_sum + lax.slice_in_dim(face_values, 1, extent, axis=along) - lax.slice_in_dim(face_values, 0, extent - 1, axis=along)
    return (cube_view - step_ratio * change_sum).reshape(plasma_state.shape)

def thread_solve(samples, conductance, lengths):
    points = samples.shape[1]
    position = jnp.arange(points, dtype=jnp.int32)[None, :]
    link_weight = jnp.where(position + 1 < lengths[:, None], conductance, jnp.zeros_like(conductance))
    before = jnp.concatenate([jnp.zeros((link_weight.shape[0], 1), jnp.float32), link_weight[:, :-1]], axis=1)
    diagonal = 1.0 + before + link_weight
    solved = lax.linalg.tridiagonal_solve(-before, diagonal, -link_weight, samples[:, :, None])
    return solved[:, :, 0]

def reference(plasma_state, jacobian, send_list, recv_map, visit_point, visit_cell, conductance, lengths):
    devices = N_SHELL * N_BLK
    fields, cells = (plasma_state.shape[0], plasma_state.shape[2])
    blocks_dev = BLOCKS // devices
    wave_speed = jnp.max(jnp.sum(jnp.abs(jacobian), axis=2), axis=1)
    step_ratio = CFL_NUMBER / jnp.max(wave_speed)
    cube_view = plasma_state.reshape(fields, N_SHELL, -1, BS, BS, BS)
    inner_layer = cube_view[:, :, :, 0]
    outer_layer = cube_view[:, :, :, BS - 1]
    lower_rim = jnp.concatenate([inner_layer[:, :1], outer_layer[:, :-1]], axis=1).reshape(fields, BLOCKS, BS, BS)
    upper_rim = jnp.concatenate([inner_layer[:, 1:], outer_layer[:, -1:]], axis=1).reshape(fields, BLOCKS, BS, BS)
    state_dev = jnp.transpose(plasma_state.reshape(fields, devices, blocks_dev, cells), (1, 0, 2, 3))
    send_dev = jnp.transpose(send_list.reshape(4, devices, PIECES), (1, 0, 2))
    pieces = lax.map(lambda pair: pack_pieces(pair[0], pair[1]), (state_dev, send_dev))
    width_row = pieces.shape[2]
    received = jnp.transpose(pieces.reshape(N_SHELL, N_BLK, N_BLK, CAP, width_row), (0, 2, 1, 3, 4)).reshape(devices, PIECES, width_row)
    recv_dev = recv_map.reshape(devices, blocks_dev * 16)
    ghosts = lax.map(lambda pair: assemble_ghosts(pair[0], pair[1], blocks_dev, fields), (received, recv_dev))
    ghosts = ghosts.reshape(BLOCKS, 4, fields, BS, BS)
    advanced = advance(plasma_state, ghosts, lower_rim, upper_rim, jacobian, wave_speed, step_ratio)
    group_points = THR_GROUP * PTS
    pressure = advanced[NF - 1].reshape(devices, -1)
    cells_dev = visit_cell.reshape(devices, -1)
    points_dev = visit_point.reshape(devices, -1)
    sampled = jnp.take_along_axis(pressure, cells_dev, axis=1)
    visited = points_dev < group_points
    group_base = (jnp.arange(devices, dtype=jnp.int32) // N_BLK * group_points)[:, None]
    global_point = jnp.where(visited, points_dev + group_base, THREADS * PTS)
    samples = jnp.zeros((THREADS * PTS,), jnp.float32).at[global_point.reshape(-1)].set(sampled.reshape(-1), mode='drop')
    thread_temp = thread_solve(samples.reshape(THREADS, PTS), conductance, lengths)
    extended = jnp.concatenate([thread_temp.reshape(-1), jnp.zeros((1,), jnp.float32)])
    returned = extended[global_point]
    updated = jnp.where(visited, returned, sampled)
    cell_base = (jnp.arange(devices, dtype=jnp.int32) * pressure.shape[1])[:, None]
    new_pressure = pressure.reshape(-1).at[(cells_dev + cell_base).reshape(-1)].set(updated.reshape(-1))
    new_state = advanced.at[NF - 1].set(new_pressure.reshape(advanced.shape[1], advanced.shape[2]))
    return (new_state, thread_temp)
```

```python
import functools

import jax
import jax.numpy as jnp
from jax import lax
from jax.experimental import pallas as pl
from jax.experimental.pallas import tpu as pltpu
from jax.sharding import PartitionSpec as P

BS = 8
FULL = 17
CFL_NUMBER = 0.3
MESH = pl.DeviceIdType.MESH
F32 = jnp.float32
BF16 = jnp.bfloat16
VMEM_BYTES = 56 * 1024 * 1024


def params(collective=None):
    if collective is None:
        return pltpu.CompilerParams(vmem_limit_bytes=VMEM_BYTES)
    return pltpu.CompilerParams(
        vmem_limit_bytes=VMEM_BYTES, collective_id=collective, has_side_effects=True
    )


def iota(shape, dim):
    return lax.broadcasted_iota(jnp.int32, shape, dim)


def one_hot(mask):
    return jnp.where(mask, 1.0, 0.0).astype(BF16)


def high_low(x):
    high = x.astype(BF16).astype(F32)
    return high, x - high


def half_roll(x):
    shape = x.shape
    return pltpu.roll(x.reshape(-1, 8, 128), 4, 1).reshape(shape)


def pack_kernel(state, jac, cidx, copt, ccode, vp, u_out, slabs, ws, wmax, table, mean):
    fields = state.shape[0]
    for f in range(fields):
        u_out[f] = state[f].T.reshape(8, 64, 128)
    speed = jnp.max(jnp.sum(jnp.abs(jac[...]), axis=2), axis=1)
    ws[...] = speed
    wmax[...] = jnp.broadcast_to(jnp.max(speed), (8, 128))
    low_half = iota((1, 1, 1, 8, 128), 3) < 4
    for j in range(4):
        if j == 0:
            face = u_out[:, :, 0:8, :]
        elif j == 1:
            face = u_out[:, :, 56:64, :]
        else:
            face = u_out[:, :, pl.ds(0 if j == 2 else 7, 8, stride=8), :]
        parts = face.reshape(8, 2, 2, 2, 8, 128)
        first, second = parts[:, :, :, 0], parts[:, :, :, 1]
        left = jnp.where(low_half, first, half_roll(second))
        right = jnp.where(low_half, half_roll(first), second)
        lanes = slice(j * 128, (j + 1) * 128)
        pairs = face.reshape(8, 4, 2, 8, 128)
        mean[...] = (pairs[:, :, 0] + pairs[:, :, 1]).reshape(256, 128)
        rest = 0.25 * (mean[pl.ds(0, 128, stride=2), :] + mean[pl.ds(1, 128, stride=2), :])
        options = [
            left[:, 0].reshape(128, 128),
            right[:, 0].reshape(128, 128),
            left[:, 1].reshape(128, 128),
            right[:, 1].reshape(128, 128),
            rest,
        ]
        for option, rows in enumerate(options):
            high, low = high_low(rows)
            table[option * 128 : (option + 1) * 128, lanes] = high.astype(BF16)
            table[640 + option * 128 : 768 + option * 128, lanes] = low.astype(BF16)

    points = vp[...]
    used = points < 256 * 512
    owner = jnp.max(jnp.where(used, points >> 12, -1), axis=1, keepdims=True)
    local = jnp.where(used, points & 4095, -1).astype(F32) + 1.0

    def pair(i, carry):
        index = cidx[pl.ds(i, 1), :]
        option = copt[pl.ds(i, 1), :]
        codes = ccode[pl.ds(i, 1), :]
        picks = one_hot(iota((512, 256), 0) == index)
        got = jnp.dot(table[...], picks, preferred_element_type=F32)
        chosen = got[0:128] + got[640:768]
        for o in range(1, 5):
            chosen = jnp.where(
                option == o, got[o * 128 : (o + 1) * 128] + got[640 + o * 128 : 768 + o * 128], chosen
            )
        for half in range(2):
            peer = 2 * i + half
            lanes = slice(half * 128, half * 128 + 128)
            slabs[peer, 0:128, :] = chosen[:, lanes]
            run = jnp.sum(jnp.where(owner == peer, local, 0.0), axis=0, keepdims=True) - 1.0
            rows = [codes[:, lanes]] + [run[:, c * 128 : (c + 1) * 128] for c in range(4)]
            rows += [jnp.zeros((3, 128), F32)]
            slabs[peer, 128:136, :] = jnp.concatenate(rows, axis=0)
        return carry

    lax.fori_loop(0, 16, pair, 0)


def exchange_kernel(
    peers, shells, slabs, u, wmax, recv, lower, upper, gmax,
    send_sem, recv_sem, rim_send, rim_recv, own_sem, shell_max, group_max, blk_max,
    ssend, srecv, bsend, brecv,
):
    me = lax.axis_index("blk")
    shell = lax.axis_index("shell")
    barrier = pltpu.get_barrier_semaphore()

    def greet(d, carry):
        pl.semaphore_signal(
            barrier, inc=1, device_id={"blk": lax.rem(me + d, peers)}, device_id_type=MESH
        )
        return carry

    lax.fori_loop(1, peers, greet, 0)
    for d in range(1, shells):
        pl.semaphore_signal(
            barrier, inc=1, device_id={"shell": lax.rem(shell + d, shells)}, device_id_type=MESH
        )
    pl.semaphore_wait(barrier, peers + shells - 2)

    def shell_copy(d):
        return pltpu.make_async_remote_copy(
            src_ref=wmax, dst_ref=shell_max.at[d], send_sem=ssend.at[d], recv_sem=srecv.at[d],
            device_id={"shell": lax.rem(shell + d, shells)}, device_id_type=MESH,
        )

    for d in range(1, shells):
        shell_copy(d).start()

    def slab_copy(d):
        return pltpu.make_async_remote_copy(
            src_ref=slabs.at[lax.rem(me + d, peers)], dst_ref=recv.at[me],
            send_sem=send_sem.at[d], recv_sem=recv_sem.at[d],
            device_id={"blk": lax.rem(me + d, peers)}, device_id_type=MESH,
        )

    def start_slab(d, carry):
        slab_copy(d).start()
        return carry

    lax.fori_loop(1, peers, start_slab, 0)
    own = pltpu.make_async_copy(slabs.at[me], recv.at[me], own_sem.at[0])
    own.start()

    def rim_up():
        return pltpu.make_async_remote_copy(
            src_ref=u.at[:, 7], dst_ref=lower, send_sem=rim_send.at[0], recv_sem=rim_recv.at[0],
            device_id={"shell": lax.rem(shell + 1, shells)}, device_id_type=MESH,
        )

    def rim_down():
        return pltpu.make_async_remote_copy(
            src_ref=u.at[:, 0], dst_ref=upper, send_sem=rim_send.at[1], recv_sem=rim_recv.at[1],
            device_id={"shell": lax.rem(shell + shells - 1, shells)}, device_id_type=MESH,
        )

    own_lower = pltpu.make_async_copy(u.at[:, 0], lower, own_sem.at[1])
    own_upper = pltpu.make_async_copy(u.at[:, 7], upper, own_sem.at[2])

    @pl.when(shell < shells - 1)
    def _():
        rim_up().start()

    @pl.when(shell > 0)
    def _():
        rim_down().start()

    @pl.when(shell == 0)
    def _():
        own_lower.start()
        own_lower.wait()

    @pl.when(shell == shells - 1)
    def _():
        own_upper.start()
        own_upper.wait()

    best = wmax[...]
    for d in range(1, shells):
        shell_copy(d).wait()
        best = jnp.maximum(best, shell_max[d])
    group_max[...] = best

    def blk_copy(d):
        return pltpu.make_async_remote_copy(
            src_ref=group_max, dst_ref=blk_max.at[d], send_sem=bsend.at[d], recv_sem=brecv.at[d],
            device_id={"blk": lax.rem(me + d, peers)}, device_id_type=MESH,
        )

    def start_blk(d, carry):
        blk_copy(d).start()
        return carry

    lax.fori_loop(1, peers, start_blk, 0)

    def wait_blk(d, value):
        blk_copy(d).wait()
        return jnp.maximum(value, blk_max[d])

    gmax[...] = lax.fori_loop(1, peers, wait_blk, best)

    def wait_slab(d, carry):
        landing = pltpu.make_async_remote_copy(
            src_ref=slabs.at[lax.rem(me + d, peers)], dst_ref=recv.at[lax.rem(me + peers - d, peers)],
            send_sem=send_sem.at[d], recv_sem=recv_sem.at[d],
            device_id={"blk": lax.rem(me + d, peers)}, device_id_type=MESH,
        )
        landing.wait()
        return carry

    lax.fori_loop(1, peers, wait_slab, 0)
    own.wait()

    @pl.when(shell < shells - 1)
    def _():
        rim_up().wait_send()

    @pl.when(shell > 0)
    def _():
        rim_up().wait_recv()
        rim_down().wait_send()

    @pl.when(shell < shells - 1)
    def _():
        rim_down().wait_recv()


def assemble(recv, tgt, acc, ghosts, spread):
    def four(i, carry):
        tiles = []
        for s in range(4):
            slab = recv[4 * i + s]
            high, low = high_low(slab[0:128])
            tiles.append(
                jnp.concatenate([low, high, slab[128:136], jnp.zeros((8, 128), F32)], axis=0).astype(BF16)
            )
        rows = jnp.concatenate(tiles, axis=1)
        for n in range(4):
            lanes = slice(n * 512, (n + 1) * 512)
            picks = one_hot(iota((512, 512), 0) + i * 512 == tgt[:, lanes])
            part = jnp.dot(rows, picks, preferred_element_type=F32)
            acc[:, lanes] = jnp.where(i == 0, part, acc[:, lanes] + part)
        return carry

    acc[...] = jnp.zeros_like(acc)
    lax.fori_loop(0, recv.shape[0] // 4, four, 0)
    low_half = iota((1, 1, 8, 128), 2) < 4
    for j in range(4):
        values, codes = [], []
        for e in range(4):
            lanes = slice((j * 4 + e) * 128, (j * 4 + e + 1) * 128)
            values.append(acc[0:128, lanes] + acc[128:256, lanes])
            codes.append(acc[256:257, lanes])
        whole = codes[0] == 16.0
        coarse = (codes[0] == 32.0).reshape(1, 1, 1, 128)
        spread[pl.ds(0, 128, stride=2), :] = values[0]
        spread[pl.ds(1, 128, stride=2), :] = values[0]
        for i in range(2):
            quads = []
            for q in (2 * i, 2 * i + 1):
                fine = jnp.zeros((128, 128), F32)
                for e in range(4):
                    fine = jnp.where(codes[e] == 1.0 + q, values[e], fine)
                quads.append(jnp.where(whole, values[q], fine).reshape(8, 2, 8, 128))
            left, right = quads
            first = jnp.where(low_half, left, half_roll(right))
            second = jnp.where(low_half, half_roll(left), right)
            repeated = spread[...].reshape(8, 4, 8, 128)[:, 2 * i : 2 * i + 2]
            first = jnp.where(coarse, repeated, first)
            second = jnp.where(coarse, repeated, second)
            for xp in range(2):
                ghosts[j, :, 4 * i + 2 * xp] = first[:, xp]
                ghosts[j, :, 4 * i + 2 * xp + 1] = second[:, xp]


def step_cells(u, lower, upper, ghosts, jac, ws, ratio, padded, advanced):
    padded[:, 1:9, 8:72, :] = u[...]
    padded[:, 0, 8:72, :] = lower[...]
    padded[:, 9, 8:72, :] = upper[...]
    padded[:, 1:9, 0:8, :] = ghosts[0]
    padded[:, 1:9, 72:80, :] = ghosts[1]
    inner = iota((2, 8, 128), 1)

    def cell(n, carry):
        r, pair = n // 4, lax.rem(n, 4)
        a = pair * 2
        own = [padded[h, r + 1, pl.ds(pl.multiple_of(a * 8 + 8, 8), 16), :].reshape(2, 8, 128) for h in range(8)]
        total = [jnp.zeros((2, 8, 128), F32) for _ in range(8)]
        for d in range(3):
            gap = []
            speed = ws[d : d + 1, :].reshape(1, 1, 128)
            for h in range(8):
                if d == 0:
                    rows = pl.ds(pl.multiple_of(a * 8 + 8, 8), 16)
                    below = padded[h, r, rows, :].reshape(2, 8, 128)
                    above = padded[h, r + 2, rows, :].reshape(2, 8, 128)
                elif d == 1:
                    below = padded[h, r + 1, pl.ds(pl.multiple_of(a * 8, 8), 16), :].reshape(2, 8, 128)
                    above = padded[h, r + 1, pl.ds(pl.multiple_of(a * 8 + 16, 8), 16), :].reshape(2, 8, 128)
                else:
                    lows = [ghosts[2, h, r, pl.ds(a + k, 1), :] for k in range(2)]
                    highs = [ghosts[3, h, r, pl.ds(a + k, 1), :] for k in range(2)]
                    lows = jnp.stack([jnp.broadcast_to(x, (8, 128)) for x in lows])
                    highs = jnp.stack([jnp.broadcast_to(x, (8, 128)) for x in highs])
                    below = jnp.where(inner == 0, lows, pltpu.roll(own[h], 1, 1))
                    above = jnp.where(inner == 7, highs, pltpu.roll(own[h], 7, 1))
                gap.append(above - below)
                total[h] = total[h] - speed * (above - 2.0 * own[h] + below)
            for g in range(8):
                for h in range(8):
                    total[g] = total[g] + jac[d, g, h : h + 1, :].reshape(1, 1, 128) * gap[h]
        for g in range(8):
            advanced[g, r, pl.ds(pl.multiple_of(a * 8, 8), 16), :] = (
                own[g] - ratio * total[g]
            ).reshape(16, 128)
        return carry

    lax.fori_loop(0, 32, cell, 0)


def sample_points(pressure, vc, samples):
    high, low = high_low(pressure)
    rows = jnp.concatenate([high, low], axis=0).astype(BF16)

    def run(i, carry):
        where_to = vc[pl.ds(i, 1), :]
        picks = one_hot(iota((512, 512), 0) == (where_to & 511))
        got = jnp.dot(rows, picks, preferred_element_type=F32)
        got = got[0:128] + got[128:256]
        block = where_to >> 9
        samples[pl.ds(i, 1), :] = jnp.sum(
            jnp.where(iota((128, 512), 0) == block, got, 0.0), axis=0, keepdims=True
        )
        return carry

    lax.fori_loop(0, 8, run, 0)


def step_kernel(
    recv, tgt, u, lower, upper, gmax, jac, ws, vc, vp,
    new_state, samples, outgoing, tidx, acc, ghosts, spread, padded, advanced,
):
    assemble(recv, tgt, acc, ghosts, spread)
    ratio = 0.5 * (CFL_NUMBER / gmax[0:1, :]).reshape(1, 1, 128)
    step_cells(u, lower, upper, ghosts, jac, ws, ratio, padded, advanced)
    for f in range(8):
        new_state[f] = advanced[f].reshape(512, 128).T
    sample_points(new_state[7], vc, samples)
    tidx[...] = recv[:, 128:136, :]
    points = vp[...]
    owner = jnp.max(jnp.where(points < 256 * 512, points >> 12, -1), axis=1, keepdims=True)
    values = samples[...]
    peer = iota((32, 512), 0)
    total = jnp.zeros((32, 512), F32)
    for run in range(8):
        total = jnp.where(peer == owner[run : run + 1, :], values[run : run + 1, :], total)
    outgoing[...] = jnp.zeros_like(outgoing)
    for c in range(4):
        outgoing[:, c, :] = total[:, c * 128 : (c + 1) * 128]


def reduce_threads(weight, rhs):
    left, right = pltpu.roll(weight, 1, 1), weight
    excess = jnp.ones_like(weight)
    points = weight.shape[1]
    stride = 1
    while stride < points:
        inv = 1.0 / (excess + left + right)
        e, r = excess * inv, rhs * inv
        back, ahead = stride, points - stride
        new_excess = excess + left * pltpu.roll(e, back, 1) + right * pltpu.roll(e, ahead, 1)
        rhs = rhs + left * pltpu.roll(r, back, 1) + right * pltpu.roll(r, ahead, 1)
        left, right = (
            left * pltpu.roll(left * inv, back, 1),
            right * pltpu.roll(right * inv, ahead, 1),
        )
        excess = new_excess
        stride *= 2
    return rhs / (excess + left + right)


def thread_kernel(
    peers, outgoing, tidx, conductance, lengths, thread_temp, returned,
    arrived, picks, rows_of, back, own_sem, send_sem, recv_sem, bsend, brecv,
):
    me = lax.axis_index("blk")
    barrier = pltpu.get_barrier_semaphore()

    def greet(d, carry):
        pl.semaphore_signal(
            barrier, inc=1, device_id={"blk": lax.rem(me + d, peers)}, device_id_type=MESH
        )
        return carry

    lax.fori_loop(1, peers, greet, 0)
    pl.semaphore_wait(barrier, peers - 1)

    def copy(src, dst, slot, ssem, rsem, d):
        peer = lax.rem(me + d, peers)
        return pltpu.make_async_remote_copy(
            src_ref=src.at[peer], dst_ref=dst.at[slot], send_sem=ssem.at[d], recv_sem=rsem.at[d],
            device_id={"blk": peer}, device_id_type=MESH,
        )

    def start(d, carry):
        copy(outgoing, arrived, me, send_sem, recv_sem, d).start()
        return carry

    lax.fori_loop(1, peers, start, 0)
    own = pltpu.make_async_copy(outgoing.at[me], arrived.at[me], own_sem.at[0])
    own.start()

    def prepare(s, carry):
        point = jnp.concatenate([tidx[s, 1 + c : 2 + c, :] for c in range(4)], axis=1).astype(jnp.int32)
        picks[s] = one_hot(iota((128, 512), 0) == (point & 127))
        row = ((point >> 7) & 3) * 8 + (point >> 9)
        rows_of[s] = jnp.broadcast_to(jnp.where(point < 0, -1, row), (8, 512))
        return carry

    lax.fori_loop(0, peers, prepare, 0)
    own.wait()

    def gather(d, total):
        s = lax.rem(me + peers - d, peers)

        @pl.when(d > 0)
        def _():
            copy(outgoing, arrived, s, send_sem, recv_sem, d).wait()

        value = jnp.concatenate([arrived[s, c : c + 1, :] for c in range(4)], axis=1)
        high, low = high_low(value)
        mask = iota((32, 512), 0) == rows_of[s, 0:1, :]
        rows = jnp.concatenate([jnp.where(mask, high, 0.0), jnp.where(mask, low, 0.0)], axis=0)
        part = lax.dot_general(
            rows.astype(BF16), picks[s], (((1,), (1,)), ((), ())), preferred_element_type=F32
        )
        return total + part

    total = lax.fori_loop(0, peers, gather, jnp.zeros((64, 128), F32))
    total = total[0:32] + total[32:64]
    rhs = jnp.concatenate([total[c * 8 : (c + 1) * 8] for c in range(4)], axis=1)
    mine = pl.ds(pl.multiple_of(me * 8, 8), 8)
    weight = jnp.where(iota((8, 512), 1) + 1 < lengths[mine, :], conductance[mine, :], 0.0)
    solved = reduce_threads(weight, rhs)
    thread_temp[...] = solved
    high, low = high_low(solved)
    table = jnp.concatenate(
        [part[:, c * 128 : (c + 1) * 128] for part in (high, low) for c in range(4)], axis=0
    ).astype(BF16)

    def answer(d, carry):
        s = lax.rem(me + d, peers)
        got = jnp.dot(table, picks[s], preferred_element_type=F32)
        got = got[0:32] + got[32:64]
        mask = iota((32, 512), 0) == rows_of[s, 0:1, :]
        line = jnp.sum(jnp.where(mask, got, 0.0), axis=0, keepdims=True)
        back[s] = jnp.concatenate(
            [line[:, c * 128 : (c + 1) * 128] for c in range(4)] + [jnp.zeros((4, 128), F32)], axis=0
        )

        @pl.when(d > 0)
        def _():
            copy(back, returned, me, bsend, brecv, d).start()

        return carry

    lax.fori_loop(0, peers, answer, 0)
    mine_back = pltpu.make_async_copy(back.at[me], returned.at[me], own_sem.at[1])
    mine_back.start()

    def finish(d, carry):
        copy(back, returned, lax.rem(me + peers - d, peers), bsend, brecv, d).wait()
        return carry

    lax.fori_loop(1, peers, finish, 0)
    mine_back.wait()


def write_kernel(old, returned, vc, vp, new):
    points = vp[...]
    used = points < 256 * 512
    owner = jnp.max(jnp.where(used, points >> 12, -1), axis=1, keepdims=True)
    values = jnp.zeros((8, 512), F32)
    for o in range(returned.shape[0]):
        line = jnp.concatenate([returned[o, c : c + 1, :] for c in range(4)], axis=1)
        values = jnp.where(owner == o, line, values)
    where_to = vc[...]
    high, low = high_low(values)
    total = jnp.zeros((384, 512), F32)
    for run in range(8):
        picks = one_hot(iota((512, 512), 0) == (where_to[run : run + 1, :] & 511))
        block = jnp.where(used, where_to >> 9, -1)[run : run + 1, :]
        mask = iota((128, 512), 0) == block
        rows = jnp.concatenate(
            [
                jnp.where(mask, high[run : run + 1, :], 0.0),
                jnp.where(mask, low[run : run + 1, :], 0.0),
                jnp.where(mask, 1.0, 0.0),
            ],
            axis=0,
        ).astype(BF16)
        total = total + lax.dot_general(
            rows, picks, (((1,), (1,)), ((), ())), preferred_element_type=F32
        )
    new[0] = jnp.where(total[256:384] > 0.5, total[0:128] + total[128:256], old[0])


def column_plan(send_list, peers):
    send = send_list.reshape(4, peers, -1)
    block, face, level, quad = send[0], send[1], send[2], send[3]
    row = jnp.where(level == 3, -1, face * 128 + block)
    option = jnp.where(level == 1, quad, jnp.where(level == 2, 4, 0))
    code = jnp.where(level == 0, 16, jnp.where(level == 1, 32, jnp.where(level == 2, 1 + quad, 0)))
    spare = jnp.full((peers, 128 - row.shape[1] - 3 * FULL), -1, jnp.int32)
    head = row[:, :FULL]
    flat = jnp.zeros_like(head)
    cidx = jnp.concatenate([row, head, head, head, spare], axis=1)
    copt = jnp.concatenate([option, flat + 1, flat + 2, flat + 3, spare], axis=1)
    ccode = jnp.concatenate([code, flat, flat, flat, spare * 0], axis=1).astype(F32)
    half = peers // 2
    return cidx.reshape(half, 256), copt.reshape(half, 256), ccode.reshape(half, 256)


def targets(recv_map, peers, cap):
    named = recv_map.reshape(-1, 4, 4).transpose(1, 2, 0)
    valid = named < peers * cap
    sender, slot = named // cap, named % cap
    column = jnp.where(valid, sender * 128 + slot, -1)
    single = jnp.sum(valid.astype(jnp.int32), axis=1, keepdims=True) == 1
    lone = jnp.max(column, axis=1, keepdims=True)
    entry = jnp.arange(4, dtype=jnp.int32)[None, :, None]
    extra = jnp.where((lone & 127) < FULL, lone + cap + FULL * (entry - 1), -1)
    column = jnp.where(single, jnp.where(entry == 0, lone, extra), column)
    return column.reshape(1, -1)


def on_device(
    plasma_state, jacobian, send_list, recv_map, visit_point, visit_cell, conductance, lengths
):
    fields, blocks, cells = plasma_state.shape
    peers, shells = lax.axis_size("blk"), lax.axis_size("shell")
    cap = send_list.shape[1] // peers
    cidx, copt, ccode = column_plan(send_list, peers)
    tgt = targets(recv_map, peers, cap)
    vp = visit_point.reshape(8, -1)
    vc = visit_cell.reshape(8, -1)
    shape = jax.ShapeDtypeStruct
    u, slabs, ws, wmax = pl.pallas_call(
        pack_kernel,
        out_shape=[
            shape((fields, 8, 64, blocks), F32),
            shape((peers, 136, 128), F32),
            shape((3, blocks), F32),
            shape((8, 128), F32),
        ],
        scratch_shapes=[pltpu.VMEM((1280, 512), BF16), pltpu.VMEM((256, 128), F32)],
        compiler_params=params(),
        name="pack",
    )(plasma_state, jacobian, cidx, copt, ccode, vp)

    vmem = pl.BlockSpec(memory_space=pltpu.VMEM)
    recv, lower, upper, gmax = pl.pallas_call(
        functools.partial(exchange_kernel, peers, shells),
        in_specs=[vmem] * 3,
        out_specs=[vmem] * 4,
        out_shape=[
            shape((peers, 136, 128), F32),
            shape((fields, 64, blocks), F32),
            shape((fields, 64, blocks), F32),
            shape((8, 128), F32),
        ],
        scratch_shapes=[
            pltpu.SemaphoreType.DMA((peers,)),
            pltpu.SemaphoreType.DMA((peers,)),
            pltpu.SemaphoreType.DMA((2,)),
            pltpu.SemaphoreType.DMA((2,)),
            pltpu.SemaphoreType.DMA((3,)),
            pltpu.VMEM((shells, 8, 128), F32),
            pltpu.VMEM((8, 128), F32),
            pltpu.VMEM((peers, 8, 128), F32),
            pltpu.SemaphoreType.DMA((shells,)),
            pltpu.SemaphoreType.DMA((shells,)),
            pltpu.SemaphoreType.DMA((peers,)),
            pltpu.SemaphoreType.DMA((peers,)),
        ],
        compiler_params=params(1),
        name="exchange",
    )(slabs, u, wmax)

    stepped, samples, outgoing, tidx = pl.pallas_call(
        step_kernel,
        out_shape=[
            shape((fields, blocks, cells), F32),
            shape((8, 512), F32),
            shape((peers, 8, 128), F32),
            shape((peers, 8, 128), F32),
        ],
        scratch_shapes=[
            pltpu.VMEM((272, 2048), F32),
            pltpu.VMEM((4, fields, 8, 8, 128), F32),
            pltpu.VMEM((256, 128), F32),
            pltpu.VMEM((fields, 10, 80, 128), F32),
            pltpu.VMEM((fields, 8, 64, 128), F32),
        ],
        compiler_params=params(),
        name="step",
    )(recv, tgt, u, lower, upper, gmax, jacobian, ws, vc, vp)

    thread_temp, returned = pl.pallas_call(
        functools.partial(thread_kernel, peers),
        in_specs=[vmem] * 4,
        out_specs=[vmem] * 2,
        out_shape=[shape((8, 512), F32), shape((peers, 8, 128), F32)],
        scratch_shapes=[
            pltpu.VMEM((peers, 8, 128), F32),
            pltpu.VMEM((peers, 128, 512), BF16),
            pltpu.VMEM((peers, 8, 512), jnp.int32),
            pltpu.VMEM((peers, 8, 128), F32),
            pltpu.SemaphoreType.DMA((2,)),
            pltpu.SemaphoreType.DMA((peers,)),
            pltpu.SemaphoreType.DMA((peers,)),
            pltpu.SemaphoreType.DMA((peers,)),
            pltpu.SemaphoreType.DMA((peers,)),
        ],
        compiler_params=params(2),
        name="threads",
    )(outgoing, tidx, conductance, lengths.reshape(-1, 1))

    plane = pl.BlockSpec((1, blocks, cells), lambda i: (fields - 1, 0, 0))
    whole = lambda shape: pl.BlockSpec(shape, lambda i: (0,) * len(shape))
    new_state = pl.pallas_call(
        write_kernel,
        grid=(1,),
        in_specs=[plane, whole((peers, 8, 128)), whole((8, 512)), whole((8, 512))],
        out_specs=plane,
        out_shape=shape((fields, blocks, cells), F32),
        input_output_aliases={0: 0},
        compiler_params=params(),
        name="write",
    )(stepped, returned, vc, vp)
    return (new_state, thread_temp)


def solution(mesh):
    in_specs = (
        P(None, ("shell", "blk"), None),
        P(None, None, None, ("shell", "blk")),
        P(None, ("shell", "blk")),
        P(("shell", "blk")),
        P(("shell", "blk")),
        P(("shell", "blk")),
        P("shell", None),
        P("shell"),
    )
    out_specs = (P(None, ("shell", "blk"), None), P(("shell", "blk"), None))
    return jax.shard_map(
        on_device, mesh=mesh, in_specs=in_specs, out_specs=out_specs, check_vma=False
    )
```

```python
import functools

import jax
import jax.numpy as jnp
from jax import lax
from jax.experimental import pallas as pl
from jax.experimental.pallas import tpu as pltpu
from jax.sharding import PartitionSpec as P

BS = 8
FULL = 17
CAP = 70
PEERS = 32
SHELLS = 4
CFL_NUMBER = 0.3
MESH = pl.DeviceIdType.MESH
F32 = jnp.float32
BF16 = jnp.bfloat16
VMEM_BYTES = 60 * 1024 * 1024


def iota(shape, dim):
    return lax.broadcasted_iota(jnp.int32, shape, dim)


def one_hot(mask):
    return jnp.where(mask, 1.0, 0.0).astype(BF16)


def high_low(x):
    high = x.astype(BF16).astype(F32)
    return high, x - high


def half_roll(x):
    shape = x.shape
    return pltpu.roll(x.reshape(-1, 8, 128), 4, 1).reshape(shape)


def rows_to_lanes(ref, *lead):
    return jnp.concatenate([ref[(*lead, slice(c, c + 1))] for c in range(4)], axis=1)


def lanes_to_rows(line):
    return [line[:, c * 128 : (c + 1) * 128] for c in range(4)]


def partner(me, n, sign):
    offset = lax.rem(11 * n, PEERS)
    dy, dz, dx = lax.div(offset, 8), lax.rem(lax.div(offset, 4), 2), lax.rem(offset, 4)
    y, z, x = lax.div(me, 8), lax.rem(lax.div(me, 4), 2), lax.rem(me, 4)
    y = lax.rem(y + 4 + sign * dy, 4)
    z = lax.rem(z + dz, 2)
    x = lax.rem(x + 4 + sign * dx, 4)
    return y * 8 + z * 4 + x


def column_plan(plan, cidx, copt, ccode):
    word = plan[...]
    row, level, quad = word & 511, (word >> 9) & 3, (word >> 11) & 3
    lane = iota(word.shape, 1)
    row = jnp.where((level == 3) | (lane >= CAP), -1, row)
    option = jnp.where(level == 1, quad, jnp.where(level == 2, 4, 0))
    code = jnp.where(level == 0, 16, jnp.where(level == 1, 32, jnp.where(level == 2, 1 + quad, 0)))
    code = jnp.where(lane < CAP, code, 0)
    index = row
    for q in range(1, 4):
        start = CAP + FULL * (q - 1)
        here = (lane >= start) & (lane < start + FULL)
        index = jnp.where(here, pltpu.roll(row, start, 1), index)
        option = jnp.where(here, q, option)
    cidx[...] = index
    copt[...] = option
    ccode[...] = code.astype(F32)


def column_targets(named, tgt):
    value = named[...]
    sender = (value * 59919) >> 22
    column = jnp.where(value < PEERS * CAP, value + sender * (128 - CAP), -1)
    for j in range(4):
        rows = [column[j * 4 + e : j * 4 + e + 1, :] for e in range(4)]
        used = [jnp.where(row >= 0, 1, 0) for row in rows]
        single = used[0] + used[1] + used[2] + used[3] == 1
        lone = jnp.maximum(jnp.maximum(rows[0], rows[1]), jnp.maximum(rows[2], rows[3]))
        for e in range(4):
            if e == 0:
                other = lone
            else:
                other = jnp.where((lone & 127) < FULL, lone + CAP + FULL * (e - 1), -1)
            lanes = slice((j * 4 + e) * 128, (j * 4 + e + 1) * 128)
            tgt[:, lanes] = jnp.where(single, other, rows[e])


def build_table(u, table, mean):
    low_half = iota((1, 1, 1, 8, 128), 3) < 4
    for j in range(4):
        if j == 0:
            face = u[:, 1:9, 8:16, :]
        elif j == 1:
            face = u[:, 1:9, 64:72, :]
        else:
            face = u[:, 1:9, pl.ds(8 if j == 2 else 15, 8, stride=8), :]
        parts = face.reshape(8, 2, 2, 2, 8, 128)
        first, second = parts[:, :, :, 0], parts[:, :, :, 1]
        left = jnp.where(low_half, first, half_roll(second))
        right = jnp.where(low_half, half_roll(first), second)
        lanes = slice(j * 128, (j + 1) * 128)
        pairs = face.reshape(8, 4, 2, 8, 128)
        mean[...] = (pairs[:, :, 0] + pairs[:, :, 1]).reshape(256, 128)
        rest = 0.25 * (mean[pl.ds(0, 128, stride=2), :] + mean[pl.ds(1, 128, stride=2), :])
        options = [
            left[:, 0].reshape(128, 128),
            right[:, 0].reshape(128, 128),
            left[:, 1].reshape(128, 128),
            right[:, 1].reshape(128, 128),
            rest,
        ]
        for option, rows in enumerate(options):
            high, low = high_low(rows)
            table[option * 128 : (option + 1) * 128, lanes] = high.astype(BF16)
            table[640 + option * 128 : 768 + option * 128, lanes] = low.astype(BF16)


def inner_step(u, jac, ws, change):
    inner = iota((2, 8, 128), 1)

    def cell(n, carry):
        r, pair = lax.div(n, 4), lax.rem(n, 4)
        a = pair * 2
        rows = pl.ds(pl.multiple_of(a * 8 + 8, 8), 16)
        own = [u[h, r + 1, rows, :].reshape(2, 8, 128) for h in range(8)]
        total = [jnp.zeros((2, 8, 128), F32) for _ in range(8)]
        for d in range(3):
            gap = []
            speed = ws[d : d + 1, :].reshape(1, 1, 128)
            for h in range(8):
                if d == 0:
                    below = u[h, r, rows, :].reshape(2, 8, 128)
                    above = u[h, r + 2, rows, :].reshape(2, 8, 128)
                elif d == 1:
                    below = u[h, r + 1, pl.ds(pl.multiple_of(a * 8, 8), 16), :].reshape(2, 8, 128)
                    above = u[h, r + 1, pl.ds(pl.multiple_of(a * 8 + 16, 8), 16), :].reshape(2, 8, 128)
                else:
                    below = jnp.where(inner == 0, 0.0, pltpu.roll(own[h], 1, 1))
                    above = jnp.where(inner == 7, 0.0, pltpu.roll(own[h], 7, 1))
                gap.append(above - below)
                total[h] = total[h] - speed * (above - 2.0 * own[h] + below)
            for g in range(8):
                for h in range(8):
                    total[g] = total[g] + jac[d, g, h : h + 1, :].reshape(1, 1, 128) * gap[h]
        for g in range(8):
            change[g, r, pl.ds(pl.multiple_of(a * 8, 8), 16), :] = total[g].reshape(16, 128)
        return carry

    lax.fori_loop(0, 32, cell, 0)


def add_ghosts(g, ghosts, jac, ws, change):
    for j in range(4):
        d = 1 + j // 2
        flux = jnp.zeros((8, 8, 128), F32)
        for h in range(8):
            flux = flux + jac[d, pl.ds(g, 1), pl.ds(h, 1), :].reshape(1, 1, 128) * ghosts[j, h]
        spread = ws[d : d + 1, :].reshape(1, 1, 128) * ghosts[j, pl.ds(g, 1)].reshape(8, 8, 128)
        part = (flux if j % 2 else -flux) - spread
        if j < 2:
            rows = pl.ds(56 * j, 8)
        else:
            rows = pl.ds(7 * (j - 2), 8, stride=8)
        here = change[pl.ds(g, 1), :, rows, :].reshape(8, 8, 128)
        change[pl.ds(g, 1), :, rows, :] = (here + part).reshape(1, 8, 8, 128)


def advance_field(g, u, change, ratio, plain):
    new = u[pl.ds(g, 1), 1:9, 8:72, :] - ratio * change[pl.ds(g, 1)]
    plain[pl.ds(g, 1)] = new.reshape(512, 128).T.reshape(1, 128, 512)


def ghost_layers(acc, ghosts, spread):
    low_half = iota((1, 1, 8, 128), 2) < 4
    for j in range(4):
        values, codes = [], []
        for e in range(4):
            lanes = slice((j * 4 + e) * 128, (j * 4 + e + 1) * 128)
            values.append(acc[0:128, lanes] + acc[128:256, lanes])
            codes.append(acc[256:257, lanes])
        whole = codes[0] == 16.0
        coarse = (codes[0] == 32.0).reshape(1, 1, 1, 128)
        spread[pl.ds(0, 128, stride=2), :] = values[0]
        spread[pl.ds(1, 128, stride=2), :] = values[0]
        for i in range(2):
            quads = []
            for q in (2 * i, 2 * i + 1):
                fine = jnp.zeros((128, 128), F32)
                for e in range(4):
                    fine = jnp.where(codes[e] == 1.0 + q, values[e], fine)
                quads.append(jnp.where(whole, values[q], fine).reshape(8, 2, 8, 128))
            left, right = quads
            first = jnp.where(low_half, left, half_roll(right))
            second = jnp.where(low_half, half_roll(left), right)
            repeated = spread[...].reshape(8, 4, 8, 128)[:, 2 * i : 2 * i + 2]
            first = jnp.where(coarse, repeated, first)
            second = jnp.where(coarse, repeated, second)
            for xp in range(2):
                ghosts[j, :, 4 * i + 2 * xp] = first[:, xp]
                ghosts[j, :, 4 * i + 2 * xp + 1] = second[:, xp]


def reduce_threads(weight, rhs):
    left, right = pltpu.roll(weight, 1, 1), weight
    excess = jnp.ones_like(weight)
    points = weight.shape[1]
    stride = 1
    while stride < points:
        inv = 1.0 / (excess + left + right)
        e, r = excess * inv, rhs * inv
        back, ahead = stride, points - stride
        new_excess = excess + left * pltpu.roll(e, back, 1) + right * pltpu.roll(e, ahead, 1)
        rhs = rhs + left * pltpu.roll(r, back, 1) + right * pltpu.roll(r, ahead, 1)
        left, right = (
            left * pltpu.roll(left * inv, back, 1),
            right * pltpu.roll(right * inv, ahead, 1),
        )
        excess = new_excess
        stride *= 2
    return rhs / (excess + left + right)


def whole_kernel(
    state, jac, plan, named, vp, vc, conductance, lengths,
    new_state, thread_temp,
    plain, u, lower, upper, table, mean, cidx, copt, ccode, tgt, slabs, recv, shell_max, own_max,
    columns, acc, ghosts, change, ws, cells, picks, rows_of, weights, outgoing, arrived, back, returned,
    state_sem, rim_send, rim_recv, shell_send, shell_recv, slab_send, slab_recv,
    out_send, out_recv, back_send, back_recv, local_sem, write_sem,
):
    me = lax.axis_index("blk")
    shell = lax.axis_index("shell")
    barrier = pltpu.get_barrier_semaphore()

    loads = [pltpu.make_async_copy(state.at[f], plain.at[f], state_sem.at[f]) for f in range(8)]
    for load in loads:
        load.start()
    weight_load = pltpu.make_async_copy(
        conductance.at[pl.ds(pl.multiple_of(me * 8, 8), 8)], weights, local_sem.at[0]
    )
    weight_load.start()

    def greet(n, carry):
        pl.semaphore_signal(barrier, inc=1, device_id={"blk": partner(me, n, 1)}, device_id_type=MESH)
        return carry

    lax.fori_loop(1, PEERS, greet, 0)
    for d in range(1, SHELLS):
        pl.semaphore_signal(
            barrier, inc=1, device_id={"shell": lax.rem(shell + d, SHELLS)}, device_id_type=MESH
        )

    speed = jnp.max(jnp.sum(jnp.abs(jac[...]), axis=2), axis=1)
    ws[...] = speed
    own_max[...] = jnp.broadcast_to(jnp.max(speed), (8, 128))
    column_plan(plan, cidx, copt, ccode)
    column_targets(named, tgt)
    u[:, :, 0:8, :] = jnp.zeros((8, 10, 8, 128), F32)
    u[:, :, 72:80, :] = jnp.zeros((8, 10, 8, 128), F32)

    for f in range(8):
        loads[f].wait()
        u[f, 1:9, 8:72, :] = plain[f].T.reshape(8, 64, 128)

    pl.semaphore_wait(barrier, PEERS + SHELLS - 2)

    def shell_copy(d):
        return pltpu.make_async_remote_copy(
            src_ref=own_max, dst_ref=shell_max.at[d], send_sem=shell_send.at[d],
            recv_sem=shell_recv.at[d],
            device_id={"shell": lax.rem(shell + d, SHELLS)}, device_id_type=MESH,
        )

    for d in range(1, SHELLS):
        shell_copy(d).start()

    def rim_up():
        return pltpu.make_async_remote_copy(
            src_ref=u.at[:, 8, 8:72], dst_ref=lower, send_sem=rim_send.at[0], recv_sem=rim_recv.at[0],
            device_id={"shell": lax.rem(shell + 1, SHELLS)}, device_id_type=MESH,
        )

    def rim_down():
        return pltpu.make_async_remote_copy(
            src_ref=u.at[:, 1, 8:72], dst_ref=upper, send_sem=rim_send.at[1], recv_sem=rim_recv.at[1],
            device_id={"shell": lax.rem(shell + SHELLS - 1, SHELLS)}, device_id_type=MESH,
        )

    @pl.when(shell < SHELLS - 1)
    def _():
        rim_up().start()

    @pl.when(shell > 0)
    def _():
        rim_down().start()

    build_table(u, table, mean)
    points = jnp.concatenate([vp[pl.ds(c, 8, stride=4), :] for c in range(4)], axis=1)
    used = points < 256 * 512
    owner = jnp.max(jnp.where(used, points >> 12, -1), axis=1, keepdims=True)
    local = jnp.where(used, points & 4095, -1).astype(F32) + 1.0
    best = own_max[...]
    for d in range(1, SHELLS):
        shell_copy(d).wait()
        best = jnp.maximum(best, shell_max[d])

    def slab_copy(n, sign):
        peer = partner(me, n, 1)
        slot = me if sign > 0 else partner(me, n, -1)
        return pltpu.make_async_remote_copy(
            src_ref=slabs.at[peer], dst_ref=recv.at[slot],
            send_sem=slab_send.at[n], recv_sem=slab_recv.at[n],
            device_id={"blk": peer}, device_id_type=MESH,
        )

    def pack(i, carry):
        pair = [partner(me, 2 * i, 1), partner(me, 2 * i + 1, 1)]
        index = jnp.concatenate([cidx[pl.ds(p, 1), :] for p in pair], axis=1)
        option = jnp.concatenate([copt[pl.ds(p, 1), :] for p in pair], axis=1)
        picked = one_hot(iota((512, 256), 0) == index)
        got = jnp.dot(table[...], picked, preferred_element_type=F32)
        chosen = got[0:128] + got[640:768]
        for o in range(1, 5):
            chosen = jnp.where(
                option == o, got[o * 128 : (o + 1) * 128] + got[640 + o * 128 : 768 + o * 128], chosen
            )
        for half in range(2):
            peer = pair[half]
            slabs[peer, 0:128, :] = chosen[:, half * 128 : half * 128 + 128]
            run = jnp.sum(jnp.where(owner == peer, local, 0.0), axis=0, keepdims=True) - 1.0
            rows = [ccode[pl.ds(peer, 1), :]] + lanes_to_rows(run) + [best[0:1, :], jnp.zeros((2, 128), F32)]
            slabs[peer, 128:136, :] = jnp.concatenate(rows, axis=0)
            if half == 0:

                @pl.when(i > 0)
                def _():
                    slab_copy(2 * i, 1).start()

            else:
                slab_copy(2 * i + 1, 1).start()
        return carry

    lax.fori_loop(0, PEERS // 2, pack, 0)
    recv[me] = slabs[me]

    @pl.when(shell > 0)
    def _():
        rim_up().wait_recv()
        u[:, 0, 8:72, :] = lower[...]

    @pl.when(shell == 0)
    def _():
        u[:, 0, 8:72, :] = u[:, 1, 8:72, :]

    @pl.when(shell < SHELLS - 1)
    def _():
        rim_down().wait_recv()
        u[:, 9, 8:72, :] = upper[...]

    @pl.when(shell == SHELLS - 1)
    def _():
        u[:, 9, 8:72, :] = u[:, 8, 8:72, :]

    inner_step(u, jac, ws, change)

    def columns_of(n, carry):
        wanted = tgt[...] - partner(me, n, -1) * 128
        columns[pl.ds(pl.multiple_of(n * 128, 128), 128), :] = one_hot(iota((128, 2048), 0) == wanted)
        return carry

    lax.fori_loop(0, PEERS, columns_of, 0)
    where_to = jnp.concatenate([vc[pl.ds(c, 8, stride=4), :] for c in range(4)], axis=1)
    for run in range(8):
        cells[run] = one_hot(iota((512, 512), 0) == (where_to[run : run + 1, :] & 511))

    def arrive(i, top):
        tiles = []
        for k in range(4):
            n = 4 * i + k
            if k == 0:

                @pl.when(i > 0)
                def _():
                    slab_copy(n, -1).wait()

            else:
                slab_copy(n, -1).wait()
            slab = recv[partner(me, n, -1)]
            high, low = high_low(slab[0:128])
            tiles.append(
                jnp.concatenate([low, high, slab[128:136], jnp.zeros((8, 128), F32)], axis=0).astype(BF16)
            )
            top = jnp.maximum(top, slab[133:134])
        rows = jnp.concatenate(tiles, axis=1)
        for n in range(4):
            lanes = slice(n * 512, (n + 1) * 512)
            part = jnp.dot(
                rows, columns[pl.ds(pl.multiple_of(i * 512, 512), 512), lanes], preferred_element_type=F32
            )
            acc[:, lanes] = acc[:, lanes] + part
        return top

    acc[...] = jnp.zeros_like(acc)
    top = lax.fori_loop(0, PEERS // 4, arrive, jnp.zeros((1, 128), F32))
    ghost_layers(acc, ghosts, spread=mean)
    ratio = (0.5 * (CFL_NUMBER / top)).reshape(1, 1, 1, 128)

    add_ghosts(7, ghosts, jac, ws, change)
    advance_field(7, u, change, ratio, plain)
    high, low = high_low(plain[7])
    rows = jnp.concatenate([high, low], axis=0).astype(BF16)
    block = where_to >> 9
    total = jnp.zeros((PEERS, 512), F32)
    for run in range(8):
        got = jnp.dot(rows, cells[run], preferred_element_type=F32)
        got = got[0:128] + got[128:256]
        line = jnp.sum(
            jnp.where(iota((128, 512), 0) == block[run : run + 1, :], got, 0.0), axis=0, keepdims=True
        )
        total = jnp.where(iota((PEERS, 512), 0) == owner[run : run + 1, :], line, total)
    outgoing[...] = jnp.zeros_like(outgoing)
    for c in range(4):
        outgoing[:, c, :] = total[:, c * 128 : (c + 1) * 128]

    def line_copy(src, dst, n, sign, ssem, rsem):
        peer = partner(me, n, 1)
        slot = me if sign > 0 else partner(me, n, -1)
        return pltpu.make_async_remote_copy(
            src_ref=src.at[peer], dst_ref=dst.at[slot], send_sem=ssem.at[n], recv_sem=rsem.at[n],
            device_id={"blk": peer}, device_id_type=MESH,
        )

    def send_out(n, carry):
        line_copy(outgoing, arrived, n, 1, out_send, out_recv).start()
        return carry

    lax.fori_loop(1, PEERS, send_out, 0)
    arrived[me] = outgoing[me]

    def prepare(i, carry):
        for k in range(4):
            lanes = slice(k * 512, (k + 1) * 512)
            s = partner(me, 4 * i + k, -1)
            point = jnp.concatenate([recv[s, 129 + c : 130 + c, :] for c in range(4)], axis=1).astype(jnp.int32)
            picks[i, :, lanes] = one_hot(iota((128, 512), 0) == (point & 127))
            row = ((point >> 7) & 3) * 8 + (point >> 9)
            rows_of[i, :, lanes] = jnp.broadcast_to(jnp.where(point < 0, -1, row), (8, 512))
        return carry

    lax.fori_loop(0, PEERS // 4, prepare, 0)

    writes = [pltpu.make_async_copy(plain.at[f], new_state.at[f], write_sem.at[f]) for f in range(8)]

    def other_field(g, carry):
        add_ghosts(g, ghosts, jac, ws, change)
        advance_field(g, u, change, ratio, plain)
        return carry

    lax.fori_loop(0, 3, other_field, 0)
    for f in range(3):
        writes[f].start()

    def collect(i, total):
        parts = []
        for k in range(4):
            n = 4 * i + k
            s = partner(me, n, -1)
            if k == 0:

                @pl.when(i > 0)
                def _():
                    line_copy(outgoing, arrived, n, -1, out_send, out_recv).wait()

            else:
                line_copy(outgoing, arrived, n, -1, out_send, out_recv).wait()
            high, low = high_low(rows_to_lanes(arrived, s))
            mask = iota((32, 512), 0) == rows_of[i, 0:1, k * 512 : (k + 1) * 512]
            parts.append(
                jnp.concatenate([jnp.where(mask, high, 0.0), jnp.where(mask, low, 0.0)], axis=0).astype(BF16)
            )
        return total + lax.dot_general(
            jnp.concatenate(parts, axis=1), picks[i], (((1,), (1,)), ((), ())), preferred_element_type=F32
        )

    total = lax.fori_loop(0, PEERS // 4, collect, jnp.zeros((64, 128), F32))
    total = total[0:32] + total[32:64]
    rhs = jnp.concatenate([total[c * 8 : (c + 1) * 8] for c in range(4)], axis=1)
    first = me * 8
    here = iota((8, 128), 1) == lax.rem(first, 128) + iota((8, 128), 0)
    length = jnp.sum(jnp.where(here, lengths[pl.ds(lax.div(first, 128), 1), :], 0), axis=1, keepdims=True)
    weight_load.wait()
    weight = jnp.where(iota((8, 512), 1) + 1 < length, weights[...], 0.0)
    solved = reduce_threads(weight, rhs)
    thread_temp[...] = solved
    high, low = high_low(solved)
    answers = jnp.concatenate(lanes_to_rows(high) + lanes_to_rows(low), axis=0).astype(BF16)

    def answer(i, carry):
        got = jnp.dot(answers, picks[i], preferred_element_type=F32)
        got = got[0:32] + got[32:64]
        mask = iota((32, 2048), 0) == rows_of[i, 0:1, :]
        line = jnp.sum(jnp.where(mask, got, 0.0), axis=0, keepdims=True)
        for k in range(4):
            n = 4 * i + k
            part = lanes_to_rows(line[:, k * 512 : (k + 1) * 512])
            back[partner(me, n, -1)] = jnp.concatenate(part + [jnp.zeros((4, 128), F32)], axis=0)
        return carry

    lax.fori_loop(0, PEERS // 4, answer, 0)

    def send_back(n, carry):
        line_copy(back, returned, n, 1, back_send, back_recv).start()
        return carry

    lax.fori_loop(1, PEERS, send_back, 0)
    returned[me] = back[me]

    lax.fori_loop(3, 7, other_field, 0)
    for f in range(3, 7):
        writes[f].start()

    visited = jnp.where(used, block, -1)
    cover = jnp.zeros((128, 512), F32)
    for run in range(8):
        mask = one_hot(iota((128, 512), 0) == visited[run : run + 1, :])
        cover = cover + lax.dot_general(
            mask, cells[run], (((1,), (1,)), ((), ())), preferred_element_type=F32
        )

    def get_back(n, carry):
        line_copy(back, returned, n, -1, back_send, back_recv).wait()
        return carry

    lax.fori_loop(1, PEERS, get_back, 0)
    values = jnp.zeros((8, 512), F32)
    for o in range(PEERS):
        values = jnp.where(owner == o, rows_to_lanes(returned, o), values)
    high, low = high_low(values)
    total = jnp.zeros((256, 512), F32)
    for run in range(8):
        mask = iota((128, 512), 0) == visited[run : run + 1, :]
        rows = jnp.concatenate(
            [jnp.where(mask, high[run : run + 1, :], 0.0), jnp.where(mask, low[run : run + 1, :], 0.0)], axis=0
        ).astype(BF16)
        total = total + lax.dot_general(
            rows, cells[run], (((1,), (1,)), ((), ())), preferred_element_type=F32
        )
    plain[7] = jnp.where(cover > 0.5, total[0:128] + total[128:256], plain[7])
    writes[7].start()
    for write in writes:
        write.wait()

    @pl.when(shell < SHELLS - 1)
    def _():
        rim_up().wait_send()

    @pl.when(shell > 0)
    def _():
        rim_down().wait_send()


def on_device(
    plasma_state, jacobian, send_list, recv_map, visit_point, visit_cell, conductance, lengths
):
    fields, blocks, cells = plasma_state.shape
    block, face, level, quad = send_list[0], send_list[1], send_list[2], send_list[3]
    plan = (block + 128 * face + 512 * level + 2048 * quad).reshape(PEERS, CAP)
    plan = jnp.pad(plan, ((0, 0), (0, 128 - CAP)))
    named = recv_map.reshape(blocks, 16).T
    shape = jax.ShapeDtypeStruct
    vmem = pl.BlockSpec(memory_space=pltpu.VMEM)
    anywhere = pl.BlockSpec(memory_space=pl.ANY)
    dma = lambda n: pltpu.SemaphoreType.DMA((n,))
    buffer = lambda *dims: pltpu.VMEM(dims, F32)
    new_state, thread_temp = pl.pallas_call(
        whole_kernel,
        in_specs=[anywhere, vmem, vmem, vmem, vmem, vmem, anywhere, vmem],
        out_specs=[anywhere, vmem],
        out_shape=[shape((fields, blocks, cells), F32), shape((8, 512), F32)],
        scratch_shapes=[
            buffer(fields, blocks, cells),
            buffer(fields, 10, 80, 128),
            buffer(fields, 64, 128),
            buffer(fields, 64, 128),
            pltpu.VMEM((1280, 512), BF16),
            buffer(256, 128),
            pltpu.VMEM((PEERS, 128), jnp.int32),
            pltpu.VMEM((PEERS, 128), jnp.int32),
            buffer(PEERS, 128),
            pltpu.VMEM((1, 2048), jnp.int32),
            buffer(PEERS, 136, 128),
            buffer(PEERS, 136, 128),
            buffer(SHELLS, 8, 128),
            buffer(8, 128),
            pltpu.VMEM((PEERS * 128, 2048), BF16),
            buffer(272, 2048),
            buffer(4, fields, 8, 8, 128),
            buffer(fields, 8, 64, 128),
            buffer(3, 128),
            pltpu.VMEM((8, 512, 512), BF16),
            pltpu.VMEM((8, 128, 2048), BF16),
            pltpu.VMEM((8, 8, 2048), jnp.int32),
            buffer(8, 512),
            buffer(PEERS, 8, 128),
            buffer(PEERS, 8, 128),
            buffer(PEERS, 8, 128),
            buffer(PEERS, 8, 128),
            dma(8), dma(2), dma(2), dma(SHELLS), dma(SHELLS), dma(PEERS), dma(PEERS),
            dma(PEERS), dma(PEERS), dma(PEERS), dma(PEERS), dma(1), dma(8),
        ],
        compiler_params=pltpu.CompilerParams(
            vmem_limit_bytes=VMEM_BYTES, collective_id=1, has_side_effects=True
        ),
        name="mhd_step",
    )(
        plasma_state, jacobian, plan, named, visit_point.reshape(-1, 128), visit_cell.reshape(-1, 128),
        conductance, lengths.reshape(-1, 128),
    )
    return (new_state, thread_temp)


def solution(mesh):
    in_specs = (
        P(None, ("shell", "blk"), None),
        P(None, None, None, ("shell", "blk")),
        P(None, ("shell", "blk")),
        P(("shell", "blk")),
        P(("shell", "blk")),
        P(("shell", "blk")),
        P("shell", None),
        P("shell"),
    )
    out_specs = (P(None, ("shell", "blk"), None), P(("shell", "blk"), None))
    return jax.shard_map(
        on_device, mesh=mesh, in_specs=in_specs, out_specs=out_specs, check_vma=False
    )
```

```python
import functools

import jax
import jax.numpy as jnp
from jax import lax
from jax.experimental import pallas as pl
from jax.experimental.pallas import tpu as pltpu
from jax.sharding import PartitionSpec as P

BS = 8
FULL = 17
CAP = 70
PEERS = 32
SHELLS = 4
EARLY = 8
CFL_NUMBER = 0.3
MESH = pl.DeviceIdType.MESH
F32 = jnp.float32
BF16 = jnp.bfloat16
VMEM_BYTES = 60 * 1024 * 1024


def iota(shape, dim):
    return lax.broadcasted_iota(jnp.int32, shape, dim)


def one_hot(mask):
    return jnp.where(mask, 1.0, 0.0).astype(BF16)


def high_low(x):
    high = x.astype(BF16).astype(F32)
    return high, x - high


def half_roll(x):
    shape = x.shape
    return pltpu.roll(x.reshape(-1, 8, 128), 4, 1).reshape(shape)


def rows_to_lanes(ref, *lead):
    return jnp.concatenate([ref[(*lead, slice(c, c + 1))] for c in range(4)], axis=1)


def lanes_to_rows(line):
    return [line[:, c * 128 : (c + 1) * 128] for c in range(4)]


def partner(me, n, sign):
    offset = lax.rem(11 * n, PEERS)
    dy, dz, dx = lax.div(offset, 8), lax.rem(lax.div(offset, 4), 2), lax.rem(offset, 4)
    y, z, x = lax.div(me, 8), lax.rem(lax.div(me, 4), 2), lax.rem(me, 4)
    y = lax.rem(y + 4 + sign * dy, 4)
    z = lax.rem(z + dz, 2)
    x = lax.rem(x + 4 + sign * dx, 4)
    return y * 8 + z * 4 + x


def column_plan(send, line, plan, cidx, copt, ccode):
    slots = PEERS * CAP
    line[:, 0:slots] = send[0:1, :] + 128 * send[1:2, :] + 512 * send[2:3, :] + 2048 * send[3:4, :]
    line[:, slots:] = jnp.zeros((1, line.shape[1] - slots), jnp.int32)
    for p in range(PEERS):
        tile, shift = p * CAP // 128 * 128, p * CAP % 128
        part = line[:, tile : tile + 256]
        plan[p : p + 1, :] = (pltpu.roll(part, 256 - shift, 1) if shift else part)[:, 0:128]
    word = plan[...]
    row, level, quad = word & 511, (word >> 9) & 3, (word >> 11) & 3
    lane = iota(word.shape, 1)
    row = jnp.where((level == 3) | (lane >= CAP), -1, row)
    option = jnp.where(level == 1, quad, jnp.where(level == 2, 4, 0))
    code = jnp.where(level == 0, 16, jnp.where(level == 1, 32, jnp.where(level == 2, 1 + quad, 0)))
    code = jnp.where(lane < CAP, code, 0)
    index = row
    for q in range(1, 4):
        start = CAP + FULL * (q - 1)
        here = (lane >= start) & (lane < start + FULL)
        index = jnp.where(here, pltpu.roll(row, start, 1), index)
        option = jnp.where(here, q, option)
    cidx[...] = index
    copt[...] = option
    ccode[...] = code.astype(F32)


def column_targets(named, tgt):
    high, low = high_low(named[...].astype(F32))
    both = jnp.concatenate([high, low, jnp.zeros((96, 128), F32)], axis=0).T.astype(BF16)
    block = iota((128, 128), 1)
    entry = iota((128, 128), 0)
    widen = one_hot((entry & 15) * 8 <= block) * one_hot((entry & 15) * 8 + 8 > block) * one_hot(entry < 32)
    wide = jnp.dot(both, widen, preferred_element_type=F32).reshape(8, 16, 128)
    phase = iota((16, 128), 1) & 7
    value = jnp.zeros((16, 128), F32)
    for k in range(8):
        value = jnp.where(phase == k, wide[k], value)
    value = value.astype(jnp.int32)
    sender = (value * 59919) >> 22
    column = jnp.where(value < PEERS * CAP, value + sender * (128 - CAP), -1)
    for j in range(4):
        rows = [column[j * 4 + e : j * 4 + e + 1, :] for e in range(4)]
        used = [jnp.where(row >= 0, 1, 0) for row in rows]
        single = used[0] + used[1] + used[2] + used[3] == 1
        lone = jnp.maximum(jnp.maximum(rows[0], rows[1]), jnp.maximum(rows[2], rows[3]))
        for e in range(4):
            if e == 0:
                other = lone
            else:
                other = jnp.where((lone & 127) < FULL, lone + CAP + FULL * (e - 1), -1)
            lanes = slice((j * 4 + e) * 128, (j * 4 + e + 1) * 128)
            tgt[:, lanes] = jnp.where(single, other, rows[e])


def build_table(u, table, mean):
    low_half = iota((1, 1, 1, 8, 128), 3) < 4
    for j in range(4):
        if j == 0:
            face = u[:, 1:9, 8:16, :]
        elif j == 1:
            face = u[:, 1:9, 64:72, :]
        else:
            face = u[:, 1:9, pl.ds(8 if j == 2 else 15, 8, stride=8), :]
        parts = face.reshape(8, 2, 2, 2, 8, 128)
        first, second = parts[:, :, :, 0], parts[:, :, :, 1]
        left = jnp.where(low_half, first, half_roll(second))
        right = jnp.where(low_half, half_roll(first), second)
        lanes = slice(j * 128, (j + 1) * 128)
        pairs = face.reshape(8, 4, 2, 8, 128)
        mean[...] = (pairs[:, :, 0] + pairs[:, :, 1]).reshape(256, 128)
        rest = 0.25 * (mean[pl.ds(0, 128, stride=2), :] + mean[pl.ds(1, 128, stride=2), :])
        options = [
            left[:, 0].reshape(128, 128),
            right[:, 0].reshape(128, 128),
            left[:, 1].reshape(128, 128),
            right[:, 1].reshape(128, 128),
            rest,
        ]
        for option, rows in enumerate(options):
            high, low = high_low(rows)
            table[option * 128 : (option + 1) * 128, lanes] = high.astype(BF16)
            table[640 + option * 128 : 768 + option * 128, lanes] = low.astype(BF16)


def inner_step(u, jac, ws, change):
    inner = iota((2, 8, 128), 1)

    def cell(n, carry):
        r, pair = lax.div(n, 4), lax.rem(n, 4)
        a = pair * 2
        rows = pl.ds(pl.multiple_of(a * 8 + 8, 8), 16)
        own = [u[h, r + 1, rows, :].reshape(2, 8, 128) for h in range(8)]
        total = [jnp.zeros((2, 8, 128), F32) for _ in range(8)]
        for d in range(3):
            gap = []
            speed = ws[d : d + 1, :].reshape(1, 1, 128)
            for h in range(8):
                if d == 0:
                    below = u[h, r, rows, :].reshape(2, 8, 128)
                    above = u[h, r + 2, rows, :].reshape(2, 8, 128)
                elif d == 1:
                    below = u[h, r + 1, pl.ds(pl.multiple_of(a * 8, 8), 16), :].reshape(2, 8, 128)
                    above = u[h, r + 1, pl.ds(pl.multiple_of(a * 8 + 16, 8), 16), :].reshape(2, 8, 128)
                else:
                    below = jnp.where(inner == 0, 0.0, pltpu.roll(own[h], 1, 1))
                    above = jnp.where(inner == 7, 0.0, pltpu.roll(own[h], 7, 1))
                gap.append(above - below)
                total[h] = total[h] - speed * (above - 2.0 * own[h] + below)
            for g in range(8):
                for h in range(8):
                    total[g] = total[g] + jac[d, g, h : h + 1, :].reshape(1, 1, 128) * gap[h]
        for g in range(8):
            change[g, r, pl.ds(pl.multiple_of(a * 8, 8), 16), :] = total[g].reshape(16, 128)
        return carry

    lax.fori_loop(0, 32, cell, 0)


def add_ghosts(g, ghosts, lower, upper, jac, ws, change):
    for side, rim in enumerate((lower, upper)):
        flux = jnp.zeros((64, 128), F32)
        for h in range(8):
            flux = flux + jac[0, pl.ds(g, 1), pl.ds(h, 1), :].reshape(1, 128) * rim[h]
        spread = ws[0:1, :] * rim[pl.ds(g, 1)].reshape(64, 128)
        part = (flux if side else -flux) - spread
        change[pl.ds(g, 1), 7 * side] = change[pl.ds(g, 1), 7 * side] + part.reshape(1, 64, 128)
    for j in range(4):
        d = 1 + j // 2
        flux = jnp.zeros((8, 8, 128), F32)
        for h in range(8):
            flux = flux + jac[d, pl.ds(g, 1), pl.ds(h, 1), :].reshape(1, 1, 128) * ghosts[j, h]
        spread = ws[d : d + 1, :].reshape(1, 1, 128) * ghosts[j, pl.ds(g, 1)].reshape(8, 8, 128)
        part = (flux if j % 2 else -flux) - spread
        if j < 2:
            rows = pl.ds(56 * j, 8)
        else:
            rows = pl.ds(7 * (j - 2), 8, stride=8)
        here = change[pl.ds(g, 1), :, rows, :].reshape(8, 8, 128)
        change[pl.ds(g, 1), :, rows, :] = (here + part).reshape(1, 8, 8, 128)


def advance_field(g, u, change, ratio, plain):
    new = u[pl.ds(g, 1), 1:9, 8:72, :] - ratio * change[pl.ds(g, 1)]
    plain[pl.ds(g, 1)] = new.reshape(512, 128).T.reshape(1, 128, 512)


def ghost_layers(acc, ghosts, spread):
    low_half = iota((1, 1, 8, 128), 2) < 4
    for j in range(4):
        values, codes = [], []
        for e in range(4):
            lanes = slice((j * 4 + e) * 128, (j * 4 + e + 1) * 128)
            values.append(acc[0:128, lanes] + acc[128:256, lanes])
            codes.append(acc[256:257, lanes])
        whole = codes[0] == 16.0
        coarse = (codes[0] == 32.0).reshape(1, 1, 1, 128)
        spread[pl.ds(0, 128, stride=2), :] = values[0]
        spread[pl.ds(1, 128, stride=2), :] = values[0]
        for i in range(2):
            quads = []
            for q in (2 * i, 2 * i + 1):
                fine = jnp.zeros((128, 128), F32)
                for e in range(4):
                    fine = jnp.where(codes[e] == 1.0 + q, values[e], fine)
                quads.append(jnp.where(whole, values[q], fine).reshape(8, 2, 8, 128))
            left, right = quads
            first = jnp.where(low_half, left, half_roll(right))
            second = jnp.where(low_half, half_roll(left), right)
            repeated = spread[...].reshape(8, 4, 8, 128)[:, 2 * i : 2 * i + 2]
            first = jnp.where(coarse, repeated, first)
            second = jnp.where(coarse, repeated, second)
            for xp in range(2):
                ghosts[j, :, 4 * i + 2 * xp] = first[:, xp]
                ghosts[j, :, 4 * i + 2 * xp + 1] = second[:, xp]


def reduce_threads(weight, rhs):
    left, right = pltpu.roll(weight, 1, 1), weight
    excess = jnp.ones_like(weight)
    points = weight.shape[1]
    stride = 1
    while stride < points:
        inv = 1.0 / (excess + left + right)
        e, r = excess * inv, rhs * inv
        back, ahead = stride, points - stride
        new_excess = excess + left * pltpu.roll(e, back, 1) + right * pltpu.roll(e, ahead, 1)
        rhs = rhs + left * pltpu.roll(r, back, 1) + right * pltpu.roll(r, ahead, 1)
        left, right = (
            left * pltpu.roll(left * inv, back, 1),
            right * pltpu.roll(right * inv, ahead, 1),
        )
        excess = new_excess
        stride *= 2
    return rhs / (excess + left + right)


def whole_kernel(
    state, jac, send, named, vp, vc, conductance, lengths,
    new_state, thread_temp,
    plain, u, lower, upper, table, mean, words, plan, cidx, copt, ccode, tgt, slabs, recv, noted, top, best_top, early_top, top_in,
    columns, acc, ghosts, change, ws, cells, picks, rows_of, weights, outgoing, arrived, back, returned,
    state_sem, rim_send, rim_recv, top_send, top_recv, early_send, early_recv, slab_send, slab_recv,
    out_send, out_recv, back_send, back_recv, local_sem, write_sem,
):
    me = lax.axis_index("blk")
    shell = lax.axis_index("shell")
    barrier = pltpu.get_barrier_semaphore()

    loads = [pltpu.make_async_copy(state.at[f], plain.at[f], state_sem.at[f]) for f in range(8)]
    for load in loads:
        load.start()
    weight_load = pltpu.make_async_copy(
        conductance.at[pl.ds(pl.multiple_of(me * 8, 8), 8)], weights, local_sem.at[0]
    )
    weight_load.start()

    def greet(n, carry):
        pl.semaphore_signal(barrier, inc=1, device_id={"blk": partner(me, n, 1)}, device_id_type=MESH)
        return carry

    lax.fori_loop(1, PEERS, greet, 0)
    for d in range(1, SHELLS):
        pl.semaphore_signal(
            barrier, inc=1, device_id={"shell": lax.rem(shell + d, SHELLS)}, device_id_type=MESH
        )

    speed = jnp.max(jnp.sum(jnp.abs(jac[...]), axis=2), axis=1)
    ws[...] = speed
    top[...] = jnp.broadcast_to(jnp.max(speed), (8, 128))
    u[:, :, 0:8, :] = jnp.zeros((8, 10, 8, 128), F32)
    u[:, :, 72:80, :] = jnp.zeros((8, 10, 8, 128), F32)
    u[:, 0, 8:72, :] = jnp.zeros((8, 64, 128), F32)
    u[:, 9, 8:72, :] = jnp.zeros((8, 64, 128), F32)

    for f in range(8):
        loads[f].wait()
        u[f, 1:9, 8:72, :] = plain[f].T.reshape(8, 64, 128)

    build_table(u, table, mean)
    column_plan(send, words, plan, cidx, copt, ccode)
    points = jnp.concatenate([vp[pl.ds(c, 8, stride=4), :] for c in range(4)], axis=1)
    used = points < 256 * 512
    owner = jnp.max(jnp.where(used, points >> 12, -1), axis=1, keepdims=True)
    local = jnp.where(used, points & 4095, -1).astype(F32) + 1.0

    def slab_copy(n, sign):
        peer = partner(me, n, 1)
        slot = me if sign > 0 else partner(me, n, -1)
        return pltpu.make_async_remote_copy(
            src_ref=slabs.at[peer], dst_ref=recv.at[slot],
            send_sem=slab_send.at[n], recv_sem=slab_recv.at[n],
            device_id={"blk": peer}, device_id_type=MESH,
        )

    def pack(i, best, send):
        pair = [partner(me, 2 * i, 1), partner(me, 2 * i + 1, 1)]
        index = jnp.concatenate([cidx[pl.ds(p, 1), :] for p in pair], axis=1)
        option = jnp.concatenate([copt[pl.ds(p, 1), :] for p in pair], axis=1)
        picked = one_hot(iota((512, 256), 0) == index)
        got = jnp.dot(table[...], picked, preferred_element_type=F32)
        chosen = got[0:128] + got[640:768]
        for o in range(1, 5):
            chosen = jnp.where(
                option == o, got[o * 128 : (o + 1) * 128] + got[640 + o * 128 : 768 + o * 128], chosen
            )
        for half in range(2):
            peer = pair[half]
            run = jnp.sum(jnp.where(owner == peer, local, 0.0), axis=0, keepdims=True) - 1.0
            none = jnp.zeros((1, 128), F32)
            rows = [none, ccode[pl.ds(peer, 1), :]] + lanes_to_rows(run) + [best, none]
            notes = jnp.concatenate([jnp.zeros((120, 128), F32)] + rows, axis=0).T
            piece = chosen[:, half * 128 : half * 128 + 128]
            slabs[peer] = jnp.where(iota((128, 128), 1) > 120, notes, piece)
            if send:
                slab_copy(2 * i + half, 1).start()

    def pack_first(i, carry):
        pack(i, carry, False)
        return carry

    def pack_rest(i, carry):
        pack(i, carry, True)
        return carry

    lax.fori_loop(0, EARLY // 2, pack_first, top[0:1, :])
    pl.semaphore_wait(barrier, PEERS + SHELLS - 2)

    def top_copy(d):
        return pltpu.make_async_remote_copy(
            src_ref=top, dst_ref=top_in.at[d], send_sem=top_send.at[d], recv_sem=top_recv.at[d],
            device_id={"shell": lax.rem(shell + d, SHELLS)}, device_id_type=MESH,
        )

    for d in range(1, SHELLS):
        top_copy(d).start()

    def rim_up():
        return pltpu.make_async_remote_copy(
            src_ref=u.at[:, 8, 8:72], dst_ref=lower, send_sem=rim_send.at[0], recv_sem=rim_recv.at[0],
            device_id={"shell": lax.rem(shell + 1, SHELLS)}, device_id_type=MESH,
        )

    def rim_down():
        return pltpu.make_async_remote_copy(
            src_ref=u.at[:, 1, 8:72], dst_ref=upper, send_sem=rim_send.at[1], recv_sem=rim_recv.at[1],
            device_id={"shell": lax.rem(shell + SHELLS - 1, SHELLS)}, device_id_type=MESH,
        )

    @pl.when(shell < SHELLS - 1)
    def _():
        rim_up().start()

    @pl.when(shell > 0)
    def _():
        rim_down().start()

    def send_early(n, carry):
        slab_copy(n, 1).start()
        return carry

    lax.fori_loop(1, EARLY, send_early, 0)
    best = top[0:1, :]
    for d in range(1, SHELLS):
        top_copy(d).wait()
        best = jnp.maximum(best, top_in[d, 0:1, :])
    best_top[...] = jnp.broadcast_to(best, (8, 128))

    def early_copy(n):
        return pltpu.make_async_remote_copy(
            src_ref=best_top, dst_ref=early_top.at[n], send_sem=early_send.at[n], recv_sem=early_recv.at[n],
            device_id={"blk": partner(me, n, 1)}, device_id_type=MESH,
        )

    def send_top(n, carry):
        early_copy(n).start()
        return carry

    lax.fori_loop(1, EARLY, send_top, 0)
    lax.fori_loop(EARLY // 2, PEERS // 2, pack_rest, best)
    recv[me] = slabs[me]

    @pl.when(shell == 0)
    def _():
        lower[...] = u[:, 1, 8:72, :]

    @pl.when(shell == SHELLS - 1)
    def _():
        upper[...] = u[:, 8, 8:72, :]

    inner_step(u, jac, ws, change)
    column_targets(named, tgt)

    def columns_of(n, carry):
        wanted = tgt[...] - partner(me, n, -1) * 128
        columns[pl.ds(pl.multiple_of(n * 128, 128), 128), :] = one_hot(iota((128, 2048), 0) == wanted)
        return carry

    lax.fori_loop(0, PEERS, columns_of, 0)
    where_to = jnp.concatenate([vc[pl.ds(c, 8, stride=4), :] for c in range(4)], axis=1)
    for run in range(8):
        cells[run] = one_hot(iota((512, 512), 0) == (where_to[run : run + 1, :] & 511))

    def arrive(i, fastest):
        tiles = []
        for k in range(4):
            n = 4 * i + k
            if k == 0:

                @pl.when(i > 0)
                def _():
                    slab_copy(n, -1).wait()

            else:
                slab_copy(n, -1).wait()
            sender = partner(me, n, -1)
            slab = recv[sender]
            note = slab.T[120:128]
            noted[sender] = note
            fastest = jnp.maximum(fastest, note[6:7])
            high, low = high_low(slab)
            tiles.append(
                jnp.concatenate([low, high, jnp.broadcast_to(note[1:2], (16, 128))], axis=0).astype(BF16)
            )
        rows = jnp.concatenate(tiles, axis=1)
        for n in range(4):
            lanes = slice(n * 512, (n + 1) * 512)
            part = jnp.dot(
                rows, columns[pl.ds(pl.multiple_of(i * 512, 512), 512), lanes], preferred_element_type=F32
            )
            acc[:, lanes] = acc[:, lanes] + part
        return fastest

    acc[...] = jnp.zeros_like(acc)
    fastest = lax.fori_loop(0, PEERS // 4, arrive, best)

    def get_top(n, carry):
        early_copy(n).wait()
        return jnp.maximum(carry, early_top[n, 0:1, :])

    fastest = lax.fori_loop(1, EARLY, get_top, fastest)

    @pl.when(shell > 0)
    def _():
        rim_up().wait_recv()

    @pl.when(shell < SHELLS - 1)
    def _():
        rim_down().wait_recv()

    ghost_layers(acc, ghosts, spread=mean)
    ratio = (0.5 * (CFL_NUMBER / fastest)).reshape(1, 1, 1, 128)

    add_ghosts(7, ghosts, lower, upper, jac, ws, change)
    advance_field(7, u, change, ratio, plain)
    high, low = high_low(plain[7])
    rows = jnp.concatenate([high, low], axis=0).astype(BF16)
    block = where_to >> 9
    total = jnp.zeros((PEERS, 512), F32)
    for run in range(8):
        got = jnp.dot(rows, cells[run], preferred_element_type=F32)
        got = got[0:128] + got[128:256]
        line = jnp.sum(
            jnp.where(iota((128, 512), 0) == block[run : run + 1, :], got, 0.0), axis=0, keepdims=True
        )
        total = jnp.where(iota((PEERS, 512), 0) == owner[run : run + 1, :], line, total)
    outgoing[...] = jnp.zeros_like(outgoing)
    for c in range(4):
        outgoing[:, c, :] = total[:, c * 128 : (c + 1) * 128]

    def line_copy(src, dst, n, sign, ssem, rsem):
        peer = partner(me, n, 1)
        slot = me if sign > 0 else partner(me, n, -1)
        return pltpu.make_async_remote_copy(
            src_ref=src.at[peer], dst_ref=dst.at[slot], send_sem=ssem.at[n], recv_sem=rsem.at[n],
            device_id={"blk": peer}, device_id_type=MESH,
        )

    def send_out(n, carry):
        line_copy(outgoing, arrived, n, 1, out_send, out_recv).start()
        return carry

    lax.fori_loop(1, PEERS, send_out, 0)
    arrived[me] = outgoing[me]

    def prepare(i, carry):
        for k in range(4):
            lanes = slice(k * 512, (k + 1) * 512)
            s = partner(me, 4 * i + k, -1)
            point = jnp.concatenate([noted[s, 2 + c : 3 + c, :] for c in range(4)], axis=1).astype(jnp.int32)
            picks[i, :, lanes] = one_hot(iota((128, 512), 0) == (point & 127))
            row = ((point >> 7) & 3) * 8 + (point >> 9)
            rows_of[i, :, lanes] = jnp.broadcast_to(jnp.where(point < 0, -1, row), (8, 512))
        return carry

    lax.fori_loop(0, PEERS // 4, prepare, 0)

    writes = [pltpu.make_async_copy(plain.at[f], new_state.at[f], write_sem.at[f]) for f in range(8)]

    def other_field(g, carry):
        add_ghosts(g, ghosts, lower, upper, jac, ws, change)
        advance_field(g, u, change, ratio, plain)
        return carry

    lax.fori_loop(0, 3, other_field, 0)
    for f in range(3):
        writes[f].start()

    def get_out(n, carry):
        line_copy(outgoing, arrived, n, -1, out_send, out_recv).wait()
        return carry

    lax.fori_loop(1, PEERS, get_out, 0)
    total = jnp.zeros((128, 64), F32)
    for i in range(PEERS // 4):
        mask = one_hot(iota((32, 2048), 0) == rows_of[i, 0:1, :])
        line = jnp.concatenate([rows_to_lanes(arrived, partner(me, 4 * i + k, -1)) for k in range(4)], axis=1)
        high, low = high_low(line)
        rows = jnp.concatenate([mask * high.astype(BF16), mask * low.astype(BF16)], axis=0)
        total = total + lax.dot_general(
            picks[i], rows, (((1,), (1,)), ((), ())), preferred_element_type=F32
        )
    total = (total[:, 0:32] + total[:, 32:64]).T
    rhs = jnp.concatenate([total[c * 8 : (c + 1) * 8] for c in range(4)], axis=1)
    first = me * 8
    here = iota((8, 128), 1) == lax.rem(first, 128) + iota((8, 128), 0)
    length = jnp.sum(jnp.where(here, lengths[pl.ds(lax.div(first, 128), 1), :], 0), axis=1, keepdims=True)
    weight_load.wait()
    weight = jnp.where(iota((8, 512), 1) + 1 < length, weights[...], 0.0)
    solved = reduce_threads(weight, rhs)
    thread_temp[...] = solved
    high, low = high_low(solved)
    answers = jnp.concatenate(lanes_to_rows(high) + lanes_to_rows(low), axis=0).astype(BF16)

    for i in range(PEERS // 4):
        got = jnp.dot(answers, picks[i], preferred_element_type=F32)
        got = got[0:32] + got[32:64]
        mask = iota((32, 2048), 0) == rows_of[i, 0:1, :]
        line = jnp.sum(jnp.where(mask, got, 0.0), axis=0, keepdims=True)
        for k in range(4):
            part = lanes_to_rows(line[:, k * 512 : (k + 1) * 512])
            back[partner(me, 4 * i + k, -1)] = jnp.concatenate(part + [jnp.zeros((4, 128), F32)], axis=0)

    def send_back(n, carry):
        line_copy(back, returned, n, 1, back_send, back_recv).start()
        return carry

    lax.fori_loop(1, PEERS, send_back, 0)
    returned[me] = back[me]

    lax.fori_loop(3, 7, other_field, 0)
    for f in range(3, 7):
        writes[f].start()

    visited = jnp.where(used, block, -1)
    cover = jnp.zeros((128, 512), F32)
    for run in range(8):
        mask = one_hot(iota((128, 512), 0) == visited[run : run + 1, :])
        cover = cover + lax.dot_general(
            mask, cells[run], (((1,), (1,)), ((), ())), preferred_element_type=F32
        )

    def get_back(n, carry):
        line_copy(back, returned, n, -1, back_send, back_recv).wait()
        return carry

    lax.fori_loop(1, PEERS, get_back, 0)
    values = jnp.zeros((8, 512), F32)
    for o in range(PEERS):
        values = jnp.where(owner == o, rows_to_lanes(returned, o), values)
    high, low = high_low(values)
    total = jnp.zeros((256, 512), F32)
    for run in range(8):
        mask = iota((128, 512), 0) == visited[run : run + 1, :]
        rows = jnp.concatenate(
            [jnp.where(mask, high[run : run + 1, :], 0.0), jnp.where(mask, low[run : run + 1, :], 0.0)], axis=0
        ).astype(BF16)
        total = total + lax.dot_general(
            rows, cells[run], (((1,), (1,)), ((), ())), preferred_element_type=F32
        )
    plain[7] = jnp.where(cover > 0.5, total[0:128] + total[128:256], plain[7])
    writes[7].start()
    for write in writes:
        write.wait()

    @pl.when(shell < SHELLS - 1)
    def _():
        rim_up().wait_send()

    @pl.when(shell > 0)
    def _():
        rim_down().wait_send()


def hand_over(state, temp, new_state, thread_temp, buffer, small, sem, out_sem):
    loads = [pltpu.make_async_copy(state.at[f], buffer.at[f], sem.at[f]) for f in range(8)]
    loads.append(pltpu.make_async_copy(temp, small, sem.at[8]))
    stores = [pltpu.make_async_copy(buffer.at[f], new_state.at[f], out_sem.at[f]) for f in range(8)]
    stores.append(pltpu.make_async_copy(small, thread_temp, out_sem.at[8]))
    for load in loads:
        load.start()
    for load, store in zip(loads, stores):
        load.wait()
        store.start()
    for store in stores:
        store.wait()


def on_device(
    plasma_state, jacobian, send_list, recv_map, visit_point, visit_cell, conductance, lengths
):
    fields, blocks, cells = plasma_state.shape
    shape = jax.ShapeDtypeStruct
    vmem = pl.BlockSpec(memory_space=pltpu.VMEM)
    anywhere = pl.BlockSpec(memory_space=pl.ANY)
    dma = lambda *dims: pltpu.SemaphoreType.DMA(dims)
    buffer = lambda *dims: pltpu.VMEM(dims, F32)
    new_state, thread_temp = pl.pallas_call(
        whole_kernel,
        in_specs=[anywhere, vmem, vmem, vmem, vmem, vmem, anywhere, vmem],
        out_specs=[anywhere, vmem],
        out_shape=[shape((fields, blocks, cells), F32), shape((8, 512), F32)],
        scratch_shapes=[
            buffer(fields, blocks, cells),
            buffer(fields, 10, 80, 128),
            buffer(fields, 64, 128),
            buffer(fields, 64, 128),
            pltpu.VMEM((1280, 512), BF16),
            buffer(256, 128),
            pltpu.VMEM((1, 2432), jnp.int32),
            pltpu.VMEM((PEERS, 128), jnp.int32),
            pltpu.VMEM((PEERS, 128), jnp.int32),
            pltpu.VMEM((PEERS, 128), jnp.int32),
            buffer(PEERS, 128),
            pltpu.VMEM((1, 2048), jnp.int32),
            buffer(PEERS, 128, 128),
            buffer(PEERS, 128, 128),
            buffer(PEERS, 8, 128),
            buffer(8, 128),
            buffer(8, 128),
            buffer(8, 8, 128),
            buffer(SHELLS, 8, 128),
            pltpu.VMEM((PEERS * 128, 2048), BF16),
            buffer(272, 2048),
            buffer(4, fields, 8, 8, 128),
            buffer(fields, 8, 64, 128),
            buffer(3, 128),
            pltpu.VMEM((8, 512, 512), BF16),
            pltpu.VMEM((8, 128, 2048), BF16),
            pltpu.VMEM((8, 8, 2048), jnp.int32),
            buffer(8, 512),
            buffer(PEERS, 8, 128),
            buffer(PEERS, 8, 128),
            buffer(PEERS, 8, 128),
            buffer(PEERS, 8, 128),
            dma(8), dma(2), dma(2), dma(SHELLS), dma(SHELLS), dma(8), dma(8), dma(PEERS), dma(PEERS),
            dma(PEERS), dma(PEERS), dma(PEERS), dma(PEERS), dma(1), dma(8),
        ],
        compiler_params=pltpu.CompilerParams(
            vmem_limit_bytes=VMEM_BYTES, collective_id=1, has_side_effects=True
        ),
        name="mhd_step",
    )(
        plasma_state, jacobian, send_list, recv_map.reshape(-1, 128), visit_point.reshape(-1, 128), visit_cell.reshape(-1, 128),
        conductance, lengths.reshape(-1, 128),
    )
    return pl.pallas_call(
        hand_over,
        in_specs=[anywhere, anywhere],
        out_specs=[anywhere, anywhere],
        out_shape=[shape((fields, blocks, cells), F32), shape((8, 512), F32)],
        scratch_shapes=[buffer(fields, blocks, cells), buffer(8, 512), dma(fields + 1), dma(fields + 1)],
        compiler_params=pltpu.CompilerParams(vmem_limit_bytes=VMEM_BYTES),
        name="hand_over",
    )(new_state, thread_temp)


def solution(mesh):
    in_specs = (
        P(None, ("shell", "blk"), None),
        P(None, None, None, ("shell", "blk")),
        P(None, ("shell", "blk")),
        P(("shell", "blk")),
        P(("shell", "blk")),
        P(("shell", "blk")),
        P("shell", None),
        P("shell"),
    )
    out_specs = (P(None, ("shell", "blk"), None), P(("shell", "blk"), None))
    return jax.shard_map(
        on_device, mesh=mesh, in_specs=in_specs, out_specs=out_specs, check_vma=False
    )
```

```python
import functools

import jax
import jax.numpy as jnp
from jax import lax
from jax.experimental import pallas as pl
from jax.experimental.pallas import tpu as pltpu
from jax.sharding import PartitionSpec as P

BS = 8
FULL = 17
CAP = 70
PEERS = 32
SHELLS = 4
EARLY = 8
CFL_NUMBER = 0.3
MESH = pl.DeviceIdType.MESH
F32 = jnp.float32
BF16 = jnp.bfloat16
VMEM_BYTES = 63000 * 1024


def iota(shape, dim):
    return lax.broadcasted_iota(jnp.int32, shape, dim)


def one_hot(mask):
    return jnp.where(mask, 1.0, 0.0).astype(BF16)


def high_low(x):
    high = x.astype(BF16).astype(F32)
    return high, x - high


def half_roll(x):
    shape = x.shape
    return pltpu.roll(x.reshape(-1, 8, 128), 4, 1).reshape(shape)


def rows_to_lanes(ref, *lead):
    return jnp.concatenate([ref[(*lead, slice(c, c + 1))] for c in range(4)], axis=1)


def lanes_to_rows(line):
    return [line[:, c * 128 : (c + 1) * 128] for c in range(4)]


def partner(me, n, sign):
    offset = lax.rem(3 * n, PEERS)
    dy, dz, dx = lax.div(offset, 8), lax.rem(lax.div(offset, 4), 2), lax.rem(offset, 4)
    y, z, x = lax.div(me, 8), lax.rem(lax.div(me, 4), 2), lax.rem(me, 4)
    y = lax.rem(y + 4 + sign * dy, 4)
    z = lax.rem(z + dz, 2)
    x = lax.rem(x + 4 + sign * dx, 4)
    return y * 8 + z * 4 + x


def column_plan(send, line, plan, cidx, copt, ccode):
    slots = PEERS * CAP
    line[:, 0:slots] = send[0:1, :] + 128 * send[1:2, :] + 512 * send[2:3, :] + 2048 * send[3:4, :]
    line[:, slots:] = jnp.zeros((1, line.shape[1] - slots), jnp.int32)
    for p in range(PEERS):
        tile, shift = p * CAP // 128 * 128, p * CAP % 128
        part = line[:, tile : tile + 256]
        plan[p : p + 1, :] = (pltpu.roll(part, 256 - shift, 1) if shift else part)[:, 0:128]
    word = plan[...]
    row, level, quad = word & 511, (word >> 9) & 3, (word >> 11) & 3
    lane = iota(word.shape, 1)
    row = jnp.where((level == 3) | (lane >= CAP), -1, row)
    option = jnp.where(level == 1, quad, jnp.where(level == 2, 4, 0))
    code = jnp.where(level == 0, 16, jnp.where(level == 1, 32, jnp.where(level == 2, 1 + quad, 0)))
    code = jnp.where(lane < CAP, code, 0)
    index = row
    for q in range(1, 4):
        start = CAP + FULL * (q - 1)
        here = (lane >= start) & (lane < start + FULL)
        index = jnp.where(here, pltpu.roll(row, start, 1), index)
        option = jnp.where(here, q, option)
    cidx[...] = index
    copt[...] = option
    ccode[...] = code.astype(F32)


def column_targets(named, tgt):
    high, low = high_low(named[...].astype(F32))
    both = jnp.concatenate([high, low, jnp.zeros((96, 128), F32)], axis=0).T.astype(BF16)
    block = iota((128, 128), 1)
    entry = iota((128, 128), 0)
    widen = one_hot((entry & 15) * 8 <= block) * one_hot((entry & 15) * 8 + 8 > block) * one_hot(entry < 32)
    wide = jnp.dot(both, widen, preferred_element_type=F32).reshape(8, 16, 128)
    phase = iota((16, 128), 1) & 7
    value = jnp.zeros((16, 128), F32)
    for k in range(8):
        value = jnp.where(phase == k, wide[k], value)
    value = value.astype(jnp.int32)
    sender = (value * 59919) >> 22
    column = jnp.where(value < PEERS * CAP, value + sender * (128 - CAP), -1)
    for j in range(4):
        rows = [column[j * 4 + e : j * 4 + e + 1, :] for e in range(4)]
        used = [jnp.where(row >= 0, 1, 0) for row in rows]
        single = used[0] + used[1] + used[2] + used[3] == 1
        lone = jnp.maximum(jnp.maximum(rows[0], rows[1]), jnp.maximum(rows[2], rows[3]))
        for e in range(4):
            if e == 0:
                other = lone
            else:
                other = jnp.where((lone & 127) < FULL, lone + CAP + FULL * (e - 1), -1)
            lanes = slice((j * 4 + e) * 128, (j * 4 + e + 1) * 128)
            tgt[:, lanes] = jnp.where(single, other, rows[e])


def build_table(u, table, mean):
    low_half = iota((1, 1, 1, 8, 128), 3) < 4
    for j in range(4):
        if j == 0:
            face = u[:, 1:9, 8:16, :]
        elif j == 1:
            face = u[:, 1:9, 64:72, :]
        else:
            face = u[:, 1:9, pl.ds(8 if j == 2 else 15, 8, stride=8), :]
        parts = face.reshape(8, 2, 2, 2, 8, 128)
        first, second = parts[:, :, :, 0], parts[:, :, :, 1]
        left = jnp.where(low_half, first, half_roll(second))
        right = jnp.where(low_half, half_roll(first), second)
        lanes = slice(j * 128, (j + 1) * 128)
        pairs = face.reshape(8, 4, 2, 8, 128)
        mean[...] = (pairs[:, :, 0] + pairs[:, :, 1]).reshape(256, 128)
        rest = 0.25 * (mean[pl.ds(0, 128, stride=2), :] + mean[pl.ds(1, 128, stride=2), :])
        options = [
            left[:, 0].reshape(128, 128),
            right[:, 0].reshape(128, 128),
            left[:, 1].reshape(128, 128),
            right[:, 1].reshape(128, 128),
            rest,
        ]
        for option, rows in enumerate(options):
            high, low = high_low(rows)
            table[option * 128 : (option + 1) * 128, lanes] = high.astype(BF16)
            table[640 + option * 128 : 768 + option * 128, lanes] = low.astype(BF16)


def inner_step(u, jac, ws, change):
    inner = iota((2, 8, 128), 1)

    def cell(n, carry):
        r, pair = lax.div(n, 4), lax.rem(n, 4)
        a = pair * 2
        rows = pl.ds(pl.multiple_of(a * 8 + 8, 8), 16)
        own = [u[h, r + 1, rows, :].reshape(2, 8, 128) for h in range(8)]
        total = [jnp.zeros((2, 8, 128), F32) for _ in range(8)]
        for d in range(3):
            gap = []
            speed = ws[d : d + 1, :].reshape(1, 1, 128)
            for h in range(8):
                if d == 0:
                    below = u[h, r, rows, :].reshape(2, 8, 128)
                    above = u[h, r + 2, rows, :].reshape(2, 8, 128)
                elif d == 1:
                    below = u[h, r + 1, pl.ds(pl.multiple_of(a * 8, 8), 16), :].reshape(2, 8, 128)
                    above = u[h, r + 1, pl.ds(pl.multiple_of(a * 8 + 16, 8), 16), :].reshape(2, 8, 128)
                else:
                    below = jnp.where(inner == 0, 0.0, pltpu.roll(own[h], 1, 1))
                    above = jnp.where(inner == 7, 0.0, pltpu.roll(own[h], 7, 1))
                gap.append(above - below)
                total[h] = total[h] - speed * (above - 2.0 * own[h] + below)
            for g in range(8):
                for h in range(8):
                    total[g] = total[g] + jac[d, g, h : h + 1, :].reshape(1, 1, 128) * gap[h]
        for g in range(8):
            change[g, r, pl.ds(pl.multiple_of(a * 8, 8), 16), :] = total[g].reshape(16, 128)
        return carry

    lax.fori_loop(0, 32, cell, 0)


def add_ghosts(g, ghosts, lower, upper, jac, ws, change):
    for side, rim in enumerate((lower, upper)):
        flux = jnp.zeros((64, 128), F32)
        for h in range(8):
            flux = flux + jac[0, pl.ds(g, 1), pl.ds(h, 1), :].reshape(1, 128) * rim[h]
        spread = ws[0:1, :] * rim[pl.ds(g, 1)].reshape(64, 128)
        part = (flux if side else -flux) - spread
        change[pl.ds(g, 1), 7 * side] = change[pl.ds(g, 1), 7 * side] + part.reshape(1, 64, 128)
    for j in range(4):
        d = 1 + j // 2
        flux = jnp.zeros((8, 8, 128), F32)
        for h in range(8):
            flux = flux + jac[d, pl.ds(g, 1), pl.ds(h, 1), :].reshape(1, 1, 128) * ghosts[j, h]
        spread = ws[d : d + 1, :].reshape(1, 1, 128) * ghosts[j, pl.ds(g, 1)].reshape(8, 8, 128)
        part = (flux if j % 2 else -flux) - spread
        if j < 2:
            rows = pl.ds(56 * j, 8)
        else:
            rows = pl.ds(7 * (j - 2), 8, stride=8)
        here = change[pl.ds(g, 1), :, rows, :].reshape(8, 8, 128)
        change[pl.ds(g, 1), :, rows, :] = (here + part).reshape(1, 8, 8, 128)


def advance_field(g, u, change, ratio, plain):
    new = u[pl.ds(g, 1), 1:9, 8:72, :] - ratio * change[pl.ds(g, 1)]
    plain[pl.ds(g, 1)] = new.reshape(512, 128).T.reshape(1, 128, 512)


def ghost_layers(acc, ghosts, spread):
    low_half = iota((1, 1, 8, 128), 2) < 4
    for j in range(4):
        values, codes = [], []
        for e in range(4):
            lanes = slice((j * 4 + e) * 128, (j * 4 + e + 1) * 128)
            values.append(acc[0:128, lanes] + acc[128:256, lanes])
            codes.append(acc[256:257, lanes])
        whole = codes[0] == 16.0
        coarse = (codes[0] == 32.0).reshape(1, 1, 1, 128)
        spread[pl.ds(0, 128, stride=2), :] = values[0]
        spread[pl.ds(1, 128, stride=2), :] = values[0]
        for i in range(2):
            quads = []
            for q in (2 * i, 2 * i + 1):
                fine = jnp.zeros((128, 128), F32)
                for e in range(4):
                    fine = jnp.where(codes[e] == 1.0 + q, values[e], fine)
                quads.append(jnp.where(whole, values[q], fine).reshape(8, 2, 8, 128))
            left, right = quads
            first = jnp.where(low_half, left, half_roll(right))
            second = jnp.where(low_half, half_roll(left), right)
            repeated = spread[...].reshape(8, 4, 8, 128)[:, 2 * i : 2 * i + 2]
            first = jnp.where(coarse, repeated, first)
            second = jnp.where(coarse, repeated, second)
            for xp in range(2):
                ghosts[j, :, 4 * i + 2 * xp] = first[:, xp]
                ghosts[j, :, 4 * i + 2 * xp + 1] = second[:, xp]


def reduce_threads(weight, rhs):
    left, right = pltpu.roll(weight, 1, 1), weight
    excess = jnp.ones_like(weight)
    points = weight.shape[1]
    stride = 1
    while stride < points:
        inv = 1.0 / (excess + left + right)
        e, r = excess * inv, rhs * inv
        back, ahead = stride, points - stride
        new_excess = excess + left * pltpu.roll(e, back, 1) + right * pltpu.roll(e, ahead, 1)
        rhs = rhs + left * pltpu.roll(r, back, 1) + right * pltpu.roll(r, ahead, 1)
        left, right = (
            left * pltpu.roll(left * inv, back, 1),
            right * pltpu.roll(right * inv, ahead, 1),
        )
        excess = new_excess
        stride *= 2
    return rhs / (excess + left + right)


def whole_kernel(
    state, jac_in, send_in, named_in, vp_in, vc_in, conductance, lengths_in,
    plain, thread_temp,
    jac, send, named, vp, vc, lengths, u, lower, upper, table, mean, words, plan, cidx, copt, ccode, tgt, slabs, recv, noted, top, best_top, early_top, top_in,
    acc, ghosts, change, ws, cells, picks, rows_of, weights, outgoing, arrived, back, returned,
    state_sem, rim_send, rim_recv, top_send, top_recv, early_send, early_recv, slab_send, slab_recv,
    out_send, out_recv, back_send, back_recv, local_sem,
):
    me = lax.axis_index("blk")
    shell = lax.axis_index("shell")
    barrier = pltpu.get_barrier_semaphore()

    def greet(n, carry):
        pl.semaphore_signal(barrier, inc=1, device_id={"blk": partner(me, n, 1)}, device_id_type=MESH)
        return carry

    lax.fori_loop(1, PEERS, greet, 0)
    for d in range(1, SHELLS):
        pl.semaphore_signal(
            barrier, inc=1, device_id={"shell": lax.rem(shell + d, SHELLS)}, device_id_type=MESH
        )

    loads = [pltpu.make_async_copy(state.at[f], plain.at[f], state_sem.at[f]) for f in range(8)]
    pairs = ((jac_in, jac), (send_in, send), (vp_in, vp), (named_in, named), (vc_in, vc), (lengths_in, lengths))
    small = [pltpu.make_async_copy(src, dst, local_sem.at[1 + i]) for i, (src, dst) in enumerate(pairs)]
    for load in small + loads:
        load.start()
    weight_load = pltpu.make_async_copy(
        conductance.at[pl.ds(pl.multiple_of(me * 8, 8), 8)], weights, local_sem.at[0]
    )
    weight_load.start()

    small[0].wait()
    speed = jnp.max(jnp.sum(jnp.abs(jac[...]), axis=2), axis=1)
    ws[...] = speed
    top[...] = jnp.broadcast_to(jnp.max(speed), (8, 128))
    u[:, :, 0:8, :] = jnp.zeros((8, 10, 8, 128), F32)
    u[:, :, 72:80, :] = jnp.zeros((8, 10, 8, 128), F32)
    u[:, 0, 8:72, :] = jnp.zeros((8, 64, 128), F32)
    u[:, 9, 8:72, :] = jnp.zeros((8, 64, 128), F32)

    for f in range(8):
        loads[f].wait()
        u[f, 1:9, 8:72, :] = plain[f].T.reshape(8, 64, 128)

    build_table(u, table, mean)
    for load in small[1:]:
        load.wait()
    column_plan(send, words, plan, cidx, copt, ccode)
    points = jnp.concatenate([vp[pl.ds(c, 8, stride=4), :] for c in range(4)], axis=1)
    used = points < 256 * 512
    owner = jnp.max(jnp.where(used, points >> 12, -1), axis=1, keepdims=True)
    local = jnp.where(used, points & 4095, -1).astype(F32) + 1.0

    def slab_copy(n):
        return pltpu.make_async_remote_copy(
            src_ref=slabs.at[n], dst_ref=recv.at[n],
            send_sem=slab_send.at[n], recv_sem=slab_recv.at[n],
            device_id={"blk": partner(me, n, 1)}, device_id_type=MESH,
        )

    def pack(i, best, send):
        pair = [partner(me, 2 * i, 1), partner(me, 2 * i + 1, 1)]
        index = jnp.concatenate([cidx[pl.ds(p, 1), :] for p in pair], axis=1)
        option = jnp.concatenate([copt[pl.ds(p, 1), :] for p in pair], axis=1)
        picked = one_hot(iota((512, 256), 0) == index)
        got = jnp.dot(table[...], picked, preferred_element_type=F32)
        chosen = got[0:128] + got[640:768]
        for o in range(1, 5):
            chosen = jnp.where(
                option == o, got[o * 128 : (o + 1) * 128] + got[640 + o * 128 : 768 + o * 128], chosen
            )
        for half in range(2):
            peer = pair[half]
            run = jnp.sum(jnp.where(owner == peer, local, 0.0), axis=0, keepdims=True) - 1.0
            none = jnp.zeros((1, 128), F32)
            rows = [none, ccode[pl.ds(peer, 1), :]] + lanes_to_rows(run) + [best, none]
            notes = jnp.concatenate([jnp.zeros((120, 128), F32)] + rows, axis=0).T
            piece = chosen[:, half * 128 : half * 128 + 128]
            slabs[2 * i + half] = jnp.where(iota((128, 128), 1) > 120, notes, piece)
            if send:
                slab_copy(2 * i + half).start()

    def pack_first(i, carry):
        pack(i, carry, False)
        return carry

    def pack_rest(i, carry):
        pack(i, carry, True)
        return carry

    lax.fori_loop(0, EARLY // 2, pack_first, top[0:1, :])
    pl.semaphore_wait(barrier, PEERS + SHELLS - 2)

    def top_copy(d):
        return pltpu.make_async_remote_copy(
            src_ref=top, dst_ref=top_in.at[d], send_sem=top_send.at[d], recv_sem=top_recv.at[d],
            device_id={"shell": lax.rem(shell + d, SHELLS)}, device_id_type=MESH,
        )

    for d in range(1, SHELLS):
        top_copy(d).start()

    def rim_up():
        return pltpu.make_async_remote_copy(
            src_ref=u.at[:, 8, 8:72], dst_ref=lower, send_sem=rim_send.at[0], recv_sem=rim_recv.at[0],
            device_id={"shell": lax.rem(shell + 1, SHELLS)}, device_id_type=MESH,
        )

    def rim_down():
        return pltpu.make_async_remote_copy(
            src_ref=u.at[:, 1, 8:72], dst_ref=upper, send_sem=rim_send.at[1], recv_sem=rim_recv.at[1],
            device_id={"shell": lax.rem(shell + SHELLS - 1, SHELLS)}, device_id_type=MESH,
        )

    @pl.when(shell < SHELLS - 1)
    def _():
        rim_up().start()

    @pl.when(shell > 0)
    def _():
        rim_down().start()

    def send_early(n, carry):
        slab_copy(n).start()
        return carry

    lax.fori_loop(1, EARLY, send_early, 0)
    best = top[0:1, :]
    for d in range(1, SHELLS):
        top_copy(d).wait()
        best = jnp.maximum(best, top_in[d, 0:1, :])
    best_top[...] = jnp.broadcast_to(best, (8, 128))

    def early_copy(n):
        return pltpu.make_async_remote_copy(
            src_ref=best_top, dst_ref=early_top.at[n], send_sem=early_send.at[n], recv_sem=early_recv.at[n],
            device_id={"blk": partner(me, n, 1)}, device_id_type=MESH,
        )

    def send_top(n, carry):
        early_copy(n).start()
        return carry

    lax.fori_loop(1, EARLY, send_top, 0)
    lax.fori_loop(EARLY // 2, PEERS // 2, pack_rest, best)
    recv[0] = slabs[0]

    @pl.when(shell == 0)
    def _():
        lower[...] = u[:, 1, 8:72, :]

    @pl.when(shell == SHELLS - 1)
    def _():
        upper[...] = u[:, 8, 8:72, :]

    inner_step(u, jac, ws, change)
    column_targets(named, tgt)

    where_to = jnp.concatenate([vc[pl.ds(c, 8, stride=4), :] for c in range(4)], axis=1)
    for run in range(8):
        cells[run] = one_hot(iota((512, 512), 0) == (where_to[run : run + 1, :] & 511))

    def arrive(i, fastest):
        tiles = []
        for k in range(4):
            n = 4 * i + k
            if k == 0:

                @pl.when(i > 0)
                def _():
                    slab_copy(n).wait()

            else:
                slab_copy(n).wait()
            slab = recv[n]
            note = slab.T[120:128]
            noted[n] = note
            fastest = jnp.maximum(fastest, note[6:7])
            high, low = high_low(slab)
            tiles.append(
                jnp.concatenate([low, high, jnp.broadcast_to(note[1:2], (16, 128))], axis=0).astype(BF16)
            )
        rows = jnp.concatenate(tiles, axis=1)
        starts = [partner(me, 4 * i + k, -1) * 128 for k in range(4)]
        for n in range(4):
            lanes = slice(n * 512, (n + 1) * 512)
            wanted = tgt[:, lanes]
            picked = [one_hot(iota((128, 512), 0) == wanted - start) for start in starts]
            part = jnp.dot(rows, jnp.concatenate(picked, axis=0), preferred_element_type=F32)
            acc[:, lanes] = acc[:, lanes] + part
        return fastest

    acc[...] = jnp.zeros_like(acc)
    fastest = lax.fori_loop(0, PEERS // 4, arrive, best)

    def get_top(n, carry):
        early_copy(n).wait()
        return jnp.maximum(carry, early_top[n, 0:1, :])

    fastest = lax.fori_loop(1, EARLY, get_top, fastest)

    @pl.when(shell > 0)
    def _():
        rim_up().wait_recv()

    @pl.when(shell < SHELLS - 1)
    def _():
        rim_down().wait_recv()

    ghost_layers(acc, ghosts, spread=mean)
    ratio = (0.5 * (CFL_NUMBER / fastest)).reshape(1, 1, 1, 128)

    add_ghosts(7, ghosts, lower, upper, jac, ws, change)
    advance_field(7, u, change, ratio, plain)
    high, low = high_low(plain[7])
    rows = jnp.concatenate([high, low], axis=0).astype(BF16)
    block = where_to >> 9
    total = jnp.zeros((PEERS, 512), F32)
    for run in range(8):
        got = jnp.dot(rows, cells[run], preferred_element_type=F32)
        got = got[0:128] + got[128:256]
        line = jnp.sum(
            jnp.where(iota((128, 512), 0) == block[run : run + 1, :], got, 0.0), axis=0, keepdims=True
        )
        total = jnp.where(iota((PEERS, 512), 0) == owner[run : run + 1, :], line, total)
    outgoing[...] = jnp.zeros_like(outgoing)
    for c in range(4):
        outgoing[:, c, :] = total[:, c * 128 : (c + 1) * 128]

    def out_copy(n):
        peer = partner(me, n, 1)
        return pltpu.make_async_remote_copy(
            src_ref=outgoing.at[peer], dst_ref=arrived.at[n], send_sem=out_send.at[n], recv_sem=out_recv.at[n],
            device_id={"blk": peer}, device_id_type=MESH,
        )

    def back_copy(n):
        return pltpu.make_async_remote_copy(
            src_ref=back.at[n], dst_ref=returned.at[n], send_sem=back_send.at[n], recv_sem=back_recv.at[n],
            device_id={"blk": partner(me, n, -1)}, device_id_type=MESH,
        )

    def send_out(n, carry):
        out_copy(n).start()
        return carry

    lax.fori_loop(1, PEERS, send_out, 0)
    arrived[0] = outgoing[me]

    def prepare(i, carry):
        for k in range(4):
            lanes = slice(k * 512, (k + 1) * 512)
            s = 4 * i + k
            point = jnp.concatenate([noted[s, 2 + c : 3 + c, :] for c in range(4)], axis=1).astype(jnp.int32)
            picks[i, :, lanes] = one_hot(iota((128, 512), 0) == (point & 127))
            row = ((point >> 7) & 3) * 8 + (point >> 9)
            rows_of[i, :, lanes] = jnp.broadcast_to(jnp.where(point < 0, -1, row), (8, 512))
        return carry

    lax.fori_loop(0, PEERS // 4, prepare, 0)


    def other_field(g, carry):
        add_ghosts(g, ghosts, lower, upper, jac, ws, change)
        advance_field(g, u, change, ratio, plain)
        return carry

    lax.fori_loop(0, 3, other_field, 0)

    def get_out(n, carry):
        out_copy(n).wait()
        return carry

    lax.fori_loop(1, PEERS, get_out, 0)
    total = jnp.zeros((128, 64), F32)
    for i in range(PEERS // 4):
        mask = one_hot(iota((32, 2048), 0) == rows_of[i, 0:1, :])
        line = jnp.concatenate([rows_to_lanes(arrived, 4 * i + k) for k in range(4)], axis=1)
        high, low = high_low(line)
        rows = jnp.concatenate([mask * high.astype(BF16), mask * low.astype(BF16)], axis=0)
        total = total + lax.dot_general(
            picks[i], rows, (((1,), (1,)), ((), ())), preferred_element_type=F32
        )
    total = (total[:, 0:32] + total[:, 32:64]).T
    rhs = jnp.concatenate([total[c * 8 : (c + 1) * 8] for c in range(4)], axis=1)
    first = me * 8
    here = iota((8, 128), 1) == lax.rem(first, 128) + iota((8, 128), 0)
    length = jnp.sum(jnp.where(here, lengths[pl.ds(lax.div(first, 128), 1), :], 0), axis=1, keepdims=True)
    weight_load.wait()
    weight = jnp.where(iota((8, 512), 1) + 1 < length, weights[...], 0.0)
    solved = reduce_threads(weight, rhs)
    thread_temp[...] = solved
    high, low = high_low(solved)
    answers = jnp.concatenate(lanes_to_rows(high) + lanes_to_rows(low), axis=0).astype(BF16)

    for i in range(PEERS // 4):
        got = jnp.dot(answers, picks[i], preferred_element_type=F32)
        got = got[0:32] + got[32:64]
        mask = iota((32, 2048), 0) == rows_of[i, 0:1, :]
        line = jnp.sum(jnp.where(mask, got, 0.0), axis=0, keepdims=True)
        for k in range(4):
            part = lanes_to_rows(line[:, k * 512 : (k + 1) * 512])
            back[4 * i + k] = jnp.concatenate(part + [jnp.zeros((4, 128), F32)], axis=0)

    def send_back(n, carry):
        back_copy(n).start()
        return carry

    lax.fori_loop(1, PEERS, send_back, 0)
    returned[0] = back[0]

    lax.fori_loop(3, 7, other_field, 0)

    visited = jnp.where(used, block, -1)
    cover = jnp.zeros((128, 512), F32)
    for run in range(8):
        mask = one_hot(iota((128, 512), 0) == visited[run : run + 1, :])
        cover = cover + lax.dot_general(
            mask, cells[run], (((1,), (1,)), ((), ())), preferred_element_type=F32
        )

    def get_back(n, carry):
        back_copy(n).wait()
        return carry

    lax.fori_loop(1, PEERS, get_back, 0)
    values = jnp.zeros((8, 512), F32)
    for n in range(PEERS):
        values = jnp.where(owner == partner(me, n, 1), rows_to_lanes(returned, n), values)
    high, low = high_low(values)
    total = jnp.zeros((256, 512), F32)
    for run in range(8):
        mask = iota((128, 512), 0) == visited[run : run + 1, :]
        rows = jnp.concatenate(
            [jnp.where(mask, high[run : run + 1, :], 0.0), jnp.where(mask, low[run : run + 1, :], 0.0)], axis=0
        ).astype(BF16)
        total = total + lax.dot_general(
            rows, cells[run], (((1,), (1,)), ((), ())), preferred_element_type=F32
        )
    plain[7] = jnp.where(cover > 0.5, total[0:128] + total[128:256], plain[7])

    @pl.when(shell < SHELLS - 1)
    def _():
        rim_up().wait_send()

    @pl.when(shell > 0)
    def _():
        rim_down().wait_send()


def hand_over(state, temp, new_state, thread_temp, sem):
    copies = [
        pltpu.make_async_copy(state, new_state, sem.at[0]),
        pltpu.make_async_copy(temp, thread_temp, sem.at[1]),
    ]
    for copy in copies:
        copy.start()
    for copy in copies:
        copy.wait()


def on_device(
    plasma_state, jacobian, send_list, recv_map, visit_point, visit_cell, conductance, lengths
):
    fields, blocks, cells = plasma_state.shape
    shape = jax.ShapeDtypeStruct
    vmem = pl.BlockSpec(memory_space=pltpu.VMEM)
    anywhere = pl.BlockSpec(memory_space=pl.ANY)
    dma = lambda *dims: pltpu.SemaphoreType.DMA(dims)
    buffer = lambda *dims: pltpu.VMEM(dims, F32)
    new_state, thread_temp = pl.pallas_call(
        whole_kernel,
        in_specs=[pl.BlockSpec(memory_space=pltpu.HBM)] * 8,
        out_specs=[vmem, vmem],
        out_shape=[pltpu.VMEM((fields, blocks, cells), F32), pltpu.VMEM((8, 512), F32)],
        scratch_shapes=[
            buffer(3, fields, fields, blocks),
            pltpu.VMEM(send_list.shape, jnp.int32),
            pltpu.VMEM((16, 128), jnp.int32),
            pltpu.VMEM((32, 128), jnp.int32),
            pltpu.VMEM((32, 128), jnp.int32),
            pltpu.VMEM((2, 128), jnp.int32),
            buffer(fields, 10, 80, 128),
            buffer(fields, 64, 128),
            buffer(fields, 64, 128),
            pltpu.VMEM((1280, 512), BF16),
            buffer(256, 128),
            pltpu.VMEM((1, 2432), jnp.int32),
            pltpu.VMEM((PEERS, 128), jnp.int32),
            pltpu.VMEM((PEERS, 128), jnp.int32),
            pltpu.VMEM((PEERS, 128), jnp.int32),
            buffer(PEERS, 128),
            pltpu.VMEM((1, 2048), jnp.int32),
            buffer(PEERS, 128, 128),
            buffer(PEERS, 128, 128),
            buffer(PEERS, 8, 128),
            buffer(8, 128),
            buffer(8, 128),
            buffer(8, 8, 128),
            buffer(SHELLS, 8, 128),
            buffer(272, 2048),
            buffer(4, fields, 8, 8, 128),
            buffer(fields, 8, 64, 128),
            buffer(3, 128),
            pltpu.VMEM((8, 512, 512), BF16),
            pltpu.VMEM((8, 128, 2048), BF16),
            pltpu.VMEM((8, 8, 2048), jnp.int32),
            buffer(8, 512),
            buffer(PEERS, 8, 128),
            buffer(PEERS, 8, 128),
            buffer(PEERS, 8, 128),
            buffer(PEERS, 8, 128),
            dma(8), dma(2), dma(2), dma(SHELLS), dma(SHELLS), dma(8), dma(8), dma(PEERS), dma(PEERS),
            dma(PEERS), dma(PEERS), dma(PEERS), dma(PEERS), dma(7),
        ],
        compiler_params=pltpu.CompilerParams(
            vmem_limit_bytes=VMEM_BYTES, collective_id=1, has_side_effects=True
        ),
        name="mhd_step",
    )(
        plasma_state, jacobian, send_list, recv_map.reshape(-1, 128), visit_point.reshape(-1, 128), visit_cell.reshape(-1, 128),
        conductance, lengths.reshape(-1, 128),
    )
    return pl.pallas_call(
        hand_over,
        in_specs=[vmem, vmem],
        out_specs=[anywhere, anywhere],
        out_shape=[shape((fields, blocks, cells), F32), shape((8, 512), F32)],
        scratch_shapes=[dma(2)],
        compiler_params=pltpu.CompilerParams(vmem_limit_bytes=4 * 1024 * 1024),
        name="hand_over",
    )(new_state, thread_temp)


def solution(mesh):
    in_specs = (
        P(None, ("shell", "blk"), None),
        P(None, None, None, ("shell", "blk")),
        P(None, ("shell", "blk")),
        P(("shell", "blk")),
        P(("shell", "blk")),
        P(("shell", "blk")),
        P("shell", None),
        P("shell"),
    )
    out_specs = (P(None, ("shell", "blk"), None), P(("shell", "blk"), None))
    return jax.shard_map(
        on_device, mesh=mesh, in_specs=in_specs, out_specs=out_specs, check_vma=False
    )
```

```python
import functools

import jax
import jax.numpy as jnp
from jax import lax
from jax.experimental import pallas as pl
from jax.experimental.pallas import tpu as pltpu
from jax.sharding import PartitionSpec as P

BS = 8
FULL = 17
CAP = 70
PEERS = 32
SHELLS = 4
EARLY = 8
CFL_NUMBER = 0.3
MESH = pl.DeviceIdType.MESH
F32 = jnp.float32
BF16 = jnp.bfloat16
VMEM_BYTES = 63000 * 1024


def iota(shape, dim):
    return lax.broadcasted_iota(jnp.int32, shape, dim)


def one_hot(mask):
    return jnp.where(mask, 1.0, 0.0).astype(BF16)


def high_low(x):
    high = x.astype(BF16).astype(F32)
    return high, x - high


def half_roll(x):
    shape = x.shape
    return pltpu.roll(x.reshape(-1, 8, 128), 4, 1).reshape(shape)


def rows_to_lanes(ref, *lead):
    return jnp.concatenate([ref[(*lead, slice(c, c + 1))] for c in range(4)], axis=1)


def lanes_to_rows(line):
    return [line[:, c * 128 : (c + 1) * 128] for c in range(4)]


def partner(me, n, sign):
    offset = lax.rem(3 * n, PEERS)
    dy, dz, dx = lax.div(offset, 8), lax.rem(lax.div(offset, 4), 2), lax.rem(offset, 4)
    y, z, x = lax.div(me, 8), lax.rem(lax.div(me, 4), 2), lax.rem(me, 4)
    y = lax.rem(y + 4 + sign * dy, 4)
    z = lax.rem(z + dz, 2)
    x = lax.rem(x + 4 + sign * dx, 4)
    return y * 8 + z * 4 + x


def hops(n):
    offset = 3 * n % PEERS
    dy, dz, dx = offset // 8, offset // 4 % 2, offset % 4
    return min(dy, 4 - dy) + 2 * dz + min(dx, 4 - dx)


NEAR_FIRST = sorted(range(PEERS), key=hops)


def column_plan(send, line, plan, cidx, copt, ccode):
    slots = PEERS * CAP
    line[:, 0:slots] = send[0:1, :] + 128 * send[1:2, :] + 512 * send[2:3, :] + 2048 * send[3:4, :]
    line[:, slots:] = jnp.zeros((1, line.shape[1] - slots), jnp.int32)
    for p in range(PEERS):
        tile, shift = p * CAP // 128 * 128, p * CAP % 128
        part = line[:, tile : tile + 256]
        plan[p : p + 1, :] = (pltpu.roll(part, 256 - shift, 1) if shift else part)[:, 0:128]
    word = plan[...]
    row, level, quad = word & 511, (word >> 9) & 3, (word >> 11) & 3
    lane = iota(word.shape, 1)
    row = jnp.where((level == 3) | (lane >= CAP), -1, row)
    option = jnp.where(level == 1, quad, jnp.where(level == 2, 4, 0))
    code = jnp.where(level == 0, 16, jnp.where(level == 1, 32, jnp.where(level == 2, 1 + quad, 0)))
    code = jnp.where(lane < CAP, code, 0)
    index = row
    for q in range(1, 4):
        start = CAP + FULL * (q - 1)
        here = (lane >= start) & (lane < start + FULL)
        index = jnp.where(here, pltpu.roll(row, start, 1), index)
        option = jnp.where(here, q, option)
    cidx[...] = index
    copt[...] = option
    ccode[...] = code.astype(F32)


def column_targets(named, tgt):
    high, low = high_low(named[...].astype(F32))
    both = jnp.concatenate([high, low, jnp.zeros((96, 128), F32)], axis=0).T.astype(BF16)
    block = iota((128, 128), 1)
    entry = iota((128, 128), 0)
    widen = one_hot((entry & 15) * 8 <= block) * one_hot((entry & 15) * 8 + 8 > block) * one_hot(entry < 32)
    wide = jnp.dot(both, widen, preferred_element_type=F32).reshape(8, 16, 128)
    phase = iota((16, 128), 1) & 7
    value = jnp.zeros((16, 128), F32)
    for k in range(8):
        value = jnp.where(phase == k, wide[k], value)
    value = value.astype(jnp.int32)
    sender = (value * 59919) >> 22
    column = jnp.where(value < PEERS * CAP, value + sender * (128 - CAP), -1)
    for j in range(4):
        rows = [column[j * 4 + e : j * 4 + e + 1, :] for e in range(4)]
        used = [jnp.where(row >= 0, 1, 0) for row in rows]
        single = used[0] + used[1] + used[2] + used[3] == 1
        lone = jnp.maximum(jnp.maximum(rows[0], rows[1]), jnp.maximum(rows[2], rows[3]))
        for e in range(4):
            if e == 0:
                other = lone
            else:
                other = jnp.where((lone & 127) < FULL, lone + CAP + FULL * (e - 1), -1)
            lanes = slice((j * 4 + e) * 128, (j * 4 + e + 1) * 128)
            tgt[:, lanes] = jnp.where(single, other, rows[e])


def build_table(u, table, mean):
    low_half = iota((1, 1, 1, 8, 128), 3) < 4
    for j in range(4):
        if j == 0:
            face = u[:, 1:9, 8:16, :]
        elif j == 1:
            face = u[:, 1:9, 64:72, :]
        else:
            face = u[:, 1:9, pl.ds(8 if j == 2 else 15, 8, stride=8), :]
        parts = face.reshape(8, 2, 2, 2, 8, 128)
        first, second = parts[:, :, :, 0], parts[:, :, :, 1]
        left = jnp.where(low_half, first, half_roll(second))
        right = jnp.where(low_half, half_roll(first), second)
        lanes = slice(j * 128, (j + 1) * 128)
        pairs = face.reshape(8, 4, 2, 8, 128)
        mean[...] = (pairs[:, :, 0] + pairs[:, :, 1]).reshape(256, 128)
        rest = 0.25 * (mean[pl.ds(0, 128, stride=2), :] + mean[pl.ds(1, 128, stride=2), :])
        options = [
            left[:, 0].reshape(128, 128),
            right[:, 0].reshape(128, 128),
            left[:, 1].reshape(128, 128),
            right[:, 1].reshape(128, 128),
            rest,
        ]
        for option, rows in enumerate(options):
            high, low = high_low(rows)
            table[option * 128 : (option + 1) * 128, lanes] = high.astype(BF16)
            table[640 + option * 128 : 768 + option * 128, lanes] = low.astype(BF16)


def inner_step(u, jac, ws, change):
    inner = iota((2, 8, 128), 1)

    def cell(n, carry):
        r, pair = lax.div(n, 4), lax.rem(n, 4)
        a = pair * 2
        rows = pl.ds(pl.multiple_of(a * 8 + 8, 8), 16)
        own = [u[h, r + 1, rows, :].reshape(2, 8, 128) for h in range(8)]
        total = [jnp.zeros((2, 8, 128), F32) for _ in range(8)]
        for d in range(3):
            gap = []
            speed = ws[d : d + 1, :].reshape(1, 1, 128)
            for h in range(8):
                if d == 0:
                    below = u[h, r, rows, :].reshape(2, 8, 128)
                    above = u[h, r + 2, rows, :].reshape(2, 8, 128)
                elif d == 1:
                    below = u[h, r + 1, pl.ds(pl.multiple_of(a * 8, 8), 16), :].reshape(2, 8, 128)
                    above = u[h, r + 1, pl.ds(pl.multiple_of(a * 8 + 16, 8), 16), :].reshape(2, 8, 128)
                else:
                    below = jnp.where(inner == 0, 0.0, pltpu.roll(own[h], 1, 1))
                    above = jnp.where(inner == 7, 0.0, pltpu.roll(own[h], 7, 1))
                gap.append(above - below)
                total[h] = total[h] - speed * (above - 2.0 * own[h] + below)
            for g in range(8):
                for h in range(8):
                    total[g] = total[g] + jac[d, g, h : h + 1, :].reshape(1, 1, 128) * gap[h]
        for g in range(8):
            change[g, r, pl.ds(pl.multiple_of(a * 8, 8), 16), :] = total[g].reshape(16, 128)
        return carry

    lax.fori_loop(0, 32, cell, 0)


def add_ghosts(g, ghosts, lower, upper, jac, ws, change):
    for side, rim in enumerate((lower, upper)):
        flux = jnp.zeros((64, 128), F32)
        for h in range(8):
            flux = flux + jac[0, pl.ds(g, 1), pl.ds(h, 1), :].reshape(1, 128) * rim[h]
        spread = ws[0:1, :] * rim[pl.ds(g, 1)].reshape(64, 128)
        part = (flux if side else -flux) - spread
        change[pl.ds(g, 1), 7 * side] = change[pl.ds(g, 1), 7 * side] + part.reshape(1, 64, 128)
    for j in range(4):
        d = 1 + j // 2
        flux = jnp.zeros((8, 8, 128), F32)
        for h in range(8):
            flux = flux + jac[d, pl.ds(g, 1), pl.ds(h, 1), :].reshape(1, 1, 128) * ghosts[j, h]
        spread = ws[d : d + 1, :].reshape(1, 1, 128) * ghosts[j, pl.ds(g, 1)].reshape(8, 8, 128)
        part = (flux if j % 2 else -flux) - spread
        if j < 2:
            rows = pl.ds(56 * j, 8)
        else:
            rows = pl.ds(7 * (j - 2), 8, stride=8)
        here = change[pl.ds(g, 1), :, rows, :].reshape(8, 8, 128)
        change[pl.ds(g, 1), :, rows, :] = (here + part).reshape(1, 8, 8, 128)


def advance_field(g, u, change, ratio, plain):
    new = u[pl.ds(g, 1), 1:9, 8:72, :] - ratio * change[pl.ds(g, 1)]
    plain[pl.ds(g, 1)] = new.reshape(512, 128).T.reshape(1, 128, 512)


def ghost_layers(acc, ghosts, spread):
    low_half = iota((1, 1, 8, 128), 2) < 4
    for j in range(4):
        values, codes = [], []
        for e in range(4):
            lanes = slice((j * 4 + e) * 128, (j * 4 + e + 1) * 128)
            values.append(acc[0:128, lanes] + acc[128:256, lanes])
            codes.append(acc[256:257, lanes])
        whole = codes[0] == 16.0
        coarse = (codes[0] == 32.0).reshape(1, 1, 1, 128)
        spread[pl.ds(0, 128, stride=2), :] = values[0]
        spread[pl.ds(1, 128, stride=2), :] = values[0]
        for i in range(2):
            quads = []
            for q in (2 * i, 2 * i + 1):
                fine = jnp.zeros((128, 128), F32)
                for e in range(4):
                    fine = jnp.where(codes[e] == 1.0 + q, values[e], fine)
                quads.append(jnp.where(whole, values[q], fine).reshape(8, 2, 8, 128))
            left, right = quads
            first = jnp.where(low_half, left, half_roll(right))
            second = jnp.where(low_half, half_roll(left), right)
            repeated = spread[...].reshape(8, 4, 8, 128)[:, 2 * i : 2 * i + 2]
            first = jnp.where(coarse, repeated, first)
            second = jnp.where(coarse, repeated, second)
            for xp in range(2):
                ghosts[j, :, 4 * i + 2 * xp] = first[:, xp]
                ghosts[j, :, 4 * i + 2 * xp + 1] = second[:, xp]


def reduce_threads(weight, rhs):
    left, right = pltpu.roll(weight, 1, 1), weight
    excess = jnp.ones_like(weight)
    points = weight.shape[1]
    stride = 1
    while stride < points:
        inv = 1.0 / (excess + left + right)
        e, r = excess * inv, rhs * inv
        back, ahead = stride, points - stride
        new_excess = excess + left * pltpu.roll(e, back, 1) + right * pltpu.roll(e, ahead, 1)
        rhs = rhs + left * pltpu.roll(r, back, 1) + right * pltpu.roll(r, ahead, 1)
        left, right = (
            left * pltpu.roll(left * inv, back, 1),
            right * pltpu.roll(right * inv, ahead, 1),
        )
        excess = new_excess
        stride *= 2
    return rhs / (excess + left + right)


def whole_kernel(
    state, jac_in, send_in, named_in, vp_in, vc_in, conductance, lengths_in,
    plain, thread_temp,
    jac, send, named, vp, vc, lengths, u, lower, upper, table, mean, words, plan, cidx, copt, ccode, tgt, slabs, recv, noted, top, best_top, early_top, top_in,
    acc, ghosts, change, ws, cells, picks, rows_of, weights, outgoing, arrived, back, returned,
    state_sem, rim_send, rim_recv, top_send, top_recv, early_send, early_recv, slab_send, slab_recv,
    out_send, out_recv, back_send, back_recv, local_sem,
):
    me = lax.axis_index("blk")
    shell = lax.axis_index("shell")
    barrier = pltpu.get_barrier_semaphore()

    def greet(n, carry):
        pl.semaphore_signal(barrier, inc=1, device_id={"blk": partner(me, n, 1)}, device_id_type=MESH)
        return carry

    lax.fori_loop(1, PEERS, greet, 0)
    for d in range(1, SHELLS):
        pl.semaphore_signal(
            barrier, inc=1, device_id={"shell": lax.rem(shell + d, SHELLS)}, device_id_type=MESH
        )

    loads = [pltpu.make_async_copy(state.at[f], plain.at[f], state_sem.at[f]) for f in range(8)]
    pairs = ((jac_in, jac), (send_in, send), (vp_in, vp), (named_in, named), (vc_in, vc), (lengths_in, lengths))
    small = [pltpu.make_async_copy(src, dst, local_sem.at[1 + i]) for i, (src, dst) in enumerate(pairs)]
    for load in small + loads:
        load.start()
    weight_load = pltpu.make_async_copy(
        conductance.at[pl.ds(pl.multiple_of(me * 8, 8), 8)], weights, local_sem.at[0]
    )
    weight_load.start()

    small[0].wait()
    speed = jnp.max(jnp.sum(jnp.abs(jac[...]), axis=2), axis=1)
    ws[...] = speed
    top[...] = jnp.broadcast_to(jnp.max(speed), (8, 128))
    u[:, :, 0:8, :] = jnp.zeros((8, 10, 8, 128), F32)
    u[:, :, 72:80, :] = jnp.zeros((8, 10, 8, 128), F32)
    u[:, 0, 8:72, :] = jnp.zeros((8, 64, 128), F32)
    u[:, 9, 8:72, :] = jnp.zeros((8, 64, 128), F32)

    for f in range(8):
        loads[f].wait()
        u[f, 1:9, 8:72, :] = plain[f].T.reshape(8, 64, 128)

    build_table(u, table, mean)
    for load in small[1:]:
        load.wait()
    column_plan(send, words, plan, cidx, copt, ccode)
    points = jnp.concatenate([vp[pl.ds(c, 8, stride=4), :] for c in range(4)], axis=1)
    used = points < 256 * 512
    owner = jnp.max(jnp.where(used, points >> 12, -1), axis=1, keepdims=True)
    local = jnp.where(used, points & 4095, -1).astype(F32) + 1.0

    def slab_copy(n):
        return pltpu.make_async_remote_copy(
            src_ref=slabs.at[n], dst_ref=recv.at[n],
            send_sem=slab_send.at[n], recv_sem=slab_recv.at[n],
            device_id={"blk": partner(me, n, 1)}, device_id_type=MESH,
        )

    def pack(i, best, send):
        pair = [partner(me, 2 * i, 1), partner(me, 2 * i + 1, 1)]
        index = jnp.concatenate([cidx[pl.ds(p, 1), :] for p in pair], axis=1)
        option = jnp.concatenate([copt[pl.ds(p, 1), :] for p in pair], axis=1)
        picked = one_hot(iota((512, 256), 0) == index)
        got = jnp.dot(table[...], picked, preferred_element_type=F32)
        chosen = got[0:128] + got[640:768]
        for o in range(1, 5):
            chosen = jnp.where(
                option == o, got[o * 128 : (o + 1) * 128] + got[640 + o * 128 : 768 + o * 128], chosen
            )
        for half in range(2):
            peer = pair[half]
            run = jnp.sum(jnp.where(owner == peer, local, 0.0), axis=0, keepdims=True) - 1.0
            none = jnp.zeros((1, 128), F32)
            rows = [none, ccode[pl.ds(peer, 1), :]] + lanes_to_rows(run) + [best, none]
            notes = jnp.concatenate([jnp.zeros((120, 128), F32)] + rows, axis=0).T
            piece = chosen[:, half * 128 : half * 128 + 128]
            slabs[2 * i + half] = jnp.where(iota((128, 128), 1) > 120, notes, piece)
            if send:
                slab_copy(2 * i + half).start()

    def pack_first(i, carry):
        pack(i, carry, False)
        return carry

    def pack_rest(i, carry):
        pack(i, carry, True)
        return carry

    lax.fori_loop(0, EARLY // 2, pack_first, top[0:1, :])
    pl.semaphore_wait(barrier, PEERS + SHELLS - 2)

    def top_copy(d):
        return pltpu.make_async_remote_copy(
            src_ref=top, dst_ref=top_in.at[d], send_sem=top_send.at[d], recv_sem=top_recv.at[d],
            device_id={"shell": lax.rem(shell + d, SHELLS)}, device_id_type=MESH,
        )

    for d in range(1, SHELLS):
        top_copy(d).start()

    def rim_up():
        return pltpu.make_async_remote_copy(
            src_ref=u.at[:, 8, 8:72], dst_ref=lower, send_sem=rim_send.at[0], recv_sem=rim_recv.at[0],
            device_id={"shell": lax.rem(shell + 1, SHELLS)}, device_id_type=MESH,
        )

    def rim_down():
        return pltpu.make_async_remote_copy(
            src_ref=u.at[:, 1, 8:72], dst_ref=upper, send_sem=rim_send.at[1], recv_sem=rim_recv.at[1],
            device_id={"shell": lax.rem(shell + SHELLS - 1, SHELLS)}, device_id_type=MESH,
        )

    @pl.when(shell < SHELLS - 1)
    def _():
        rim_up().start()

    @pl.when(shell > 0)
    def _():
        rim_down().start()

    def send_early(n, carry):
        slab_copy(n).start()
        return carry

    lax.fori_loop(1, EARLY, send_early, 0)
    best = top[0:1, :]
    for d in range(1, SHELLS):
        top_copy(d).wait()
        best = jnp.maximum(best, top_in[d, 0:1, :])
    best_top[...] = jnp.broadcast_to(best, (8, 128))

    def early_copy(n):
        return pltpu.make_async_remote_copy(
            src_ref=best_top, dst_ref=early_top.at[n], send_sem=early_send.at[n], recv_sem=early_recv.at[n],
            device_id={"blk": partner(me, n, 1)}, device_id_type=MESH,
        )

    def send_top(n, carry):
        early_copy(n).start()
        return carry

    lax.fori_loop(1, EARLY, send_top, 0)
    lax.fori_loop(EARLY // 2, PEERS // 2, pack_rest, best)
    recv[0] = slabs[0]

    @pl.when(shell == 0)
    def _():
        lower[...] = u[:, 1, 8:72, :]

    @pl.when(shell == SHELLS - 1)
    def _():
        upper[...] = u[:, 8, 8:72, :]

    inner_step(u, jac, ws, change)
    column_targets(named, tgt)

    where_to = jnp.concatenate([vc[pl.ds(c, 8, stride=4), :] for c in range(4)], axis=1)
    for run in range(8):
        cells[run] = one_hot(iota((512, 512), 0) == (where_to[run : run + 1, :] & 511))

    def arrive(i, fastest):
        tiles = []
        for k in range(4):
            n = 4 * i + k
            if k == 0:

                @pl.when(i > 0)
                def _():
                    slab_copy(n).wait()

            else:
                slab_copy(n).wait()
            slab = recv[n]
            note = slab.T[120:128]
            noted[n] = note
            fastest = jnp.maximum(fastest, note[6:7])
            high, low = high_low(slab)
            tiles.append(
                jnp.concatenate([low, high, jnp.broadcast_to(note[1:2], (16, 128))], axis=0).astype(BF16)
            )
        rows = jnp.concatenate(tiles, axis=1)
        starts = [partner(me, 4 * i + k, -1) * 128 for k in range(4)]
        for n in range(4):
            lanes = slice(n * 512, (n + 1) * 512)
            wanted = tgt[:, lanes]
            picked = [one_hot(iota((128, 512), 0) == wanted - start) for start in starts]
            part = jnp.dot(rows, jnp.concatenate(picked, axis=0), preferred_element_type=F32)
            acc[:, lanes] = acc[:, lanes] + part
        return fastest

    acc[...] = jnp.zeros_like(acc)
    fastest = lax.fori_loop(0, PEERS // 4, arrive, best)

    def get_top(n, carry):
        early_copy(n).wait()
        return jnp.maximum(carry, early_top[n, 0:1, :])

    fastest = lax.fori_loop(1, EARLY, get_top, fastest)

    @pl.when(shell > 0)
    def _():
        rim_up().wait_recv()

    @pl.when(shell < SHELLS - 1)
    def _():
        rim_down().wait_recv()

    ghost_layers(acc, ghosts, spread=mean)
    ratio = (0.5 * (CFL_NUMBER / fastest)).reshape(1, 1, 1, 128)

    add_ghosts(7, ghosts, lower, upper, jac, ws, change)
    advance_field(7, u, change, ratio, plain)
    high, low = high_low(plain[7])
    rows = jnp.concatenate([high, low], axis=0).astype(BF16)
    block = where_to >> 9
    total = jnp.zeros((PEERS, 512), F32)
    for run in range(8):
        got = jnp.dot(rows, cells[run], preferred_element_type=F32)
        got = got[0:128] + got[128:256]
        line = jnp.sum(
            jnp.where(iota((128, 512), 0) == block[run : run + 1, :], got, 0.0), axis=0, keepdims=True
        )
        total = jnp.where(iota((PEERS, 512), 0) == owner[run : run + 1, :], line, total)
    outgoing[...] = jnp.zeros_like(outgoing)
    for c in range(4):
        outgoing[:, c, :] = total[:, c * 128 : (c + 1) * 128]

    def out_copy(n):
        peer = partner(me, n, 1)
        return pltpu.make_async_remote_copy(
            src_ref=outgoing.at[peer], dst_ref=arrived.at[n], send_sem=out_send.at[n], recv_sem=out_recv.at[n],
            device_id={"blk": peer}, device_id_type=MESH,
        )

    def back_copy(n):
        return pltpu.make_async_remote_copy(
            src_ref=back.at[n], dst_ref=returned.at[n], send_sem=back_send.at[n], recv_sem=back_recv.at[n],
            device_id={"blk": partner(me, n, -1)}, device_id_type=MESH,
        )

    def send_out(n, carry):
        out_copy(n).start()
        return carry

    lax.fori_loop(1, PEERS, send_out, 0)
    arrived[0] = outgoing[me]

    for place, n in enumerate(NEAR_FIRST):
        i, lanes = place // 4, slice(place % 4 * 512, (place % 4 + 1) * 512)
        point = jnp.concatenate([noted[n, 2 + c : 3 + c, :] for c in range(4)], axis=1).astype(jnp.int32)
        picks[i, :, lanes] = one_hot(iota((128, 512), 0) == (point & 127))
        row = ((point >> 7) & 3) * 8 + (point >> 9)
        rows_of[i, :, lanes] = jnp.broadcast_to(jnp.where(point < 0, -1, row), (8, 512))


    def other_field(g, carry):
        add_ghosts(g, ghosts, lower, upper, jac, ws, change)
        advance_field(g, u, change, ratio, plain)
        return carry

    lax.fori_loop(0, 3, other_field, 0)

    total = jnp.zeros((128, 64), F32)
    for i in range(PEERS // 4):
        near = NEAR_FIRST[4 * i : 4 * i + 4]
        for n in near:
            if n:
                out_copy(n).wait()
        mask = one_hot(iota((32, 2048), 0) == rows_of[i, 0:1, :])
        line = jnp.concatenate([rows_to_lanes(arrived, n) for n in near], axis=1)
        high, low = high_low(line)
        rows = jnp.concatenate([mask * high.astype(BF16), mask * low.astype(BF16)], axis=0)
        total = total + lax.dot_general(
            picks[i], rows, (((1,), (1,)), ((), ())), preferred_element_type=F32
        )
    total = (total[:, 0:32] + total[:, 32:64]).T
    rhs = jnp.concatenate([total[c * 8 : (c + 1) * 8] for c in range(4)], axis=1)
    first = me * 8
    here = iota((8, 128), 1) == lax.rem(first, 128) + iota((8, 128), 0)
    length = jnp.sum(jnp.where(here, lengths[pl.ds(lax.div(first, 128), 1), :], 0), axis=1, keepdims=True)
    weight_load.wait()
    weight = jnp.where(iota((8, 512), 1) + 1 < length, weights[...], 0.0)
    solved = reduce_threads(weight, rhs)
    thread_temp[...] = solved
    high, low = high_low(solved)
    answers = jnp.concatenate(lanes_to_rows(high) + lanes_to_rows(low), axis=0).astype(BF16)

    for i in reversed(range(PEERS // 4)):
        got = jnp.dot(answers, picks[i], preferred_element_type=F32)
        got = got[0:32] + got[32:64]
        mask = iota((32, 2048), 0) == rows_of[i, 0:1, :]
        line = jnp.sum(jnp.where(mask, got, 0.0), axis=0, keepdims=True)
        for k in range(4):
            part = lanes_to_rows(line[:, k * 512 : (k + 1) * 512])
            n = NEAR_FIRST[4 * i + k]
            back[n] = jnp.concatenate(part + [jnp.zeros((4, 128), F32)], axis=0)
            if n:
                back_copy(n).start()

    returned[0] = back[0]

    lax.fori_loop(3, 7, other_field, 0)

    visited = jnp.where(used, block, -1)
    cover = jnp.zeros((128, 512), F32)
    for run in range(8):
        mask = one_hot(iota((128, 512), 0) == visited[run : run + 1, :])
        cover = cover + lax.dot_general(
            mask, cells[run], (((1,), (1,)), ((), ())), preferred_element_type=F32
        )

    def get_back(n, carry):
        back_copy(n).wait()
        return carry

    lax.fori_loop(1, PEERS, get_back, 0)
    values = jnp.zeros((8, 512), F32)
    for n in range(PEERS):
        values = jnp.where(owner == partner(me, n, 1), rows_to_lanes(returned, n), values)
    high, low = high_low(values)
    total = jnp.zeros((256, 512), F32)
    for run in range(8):
        mask = iota((128, 512), 0) == visited[run : run + 1, :]
        rows = jnp.concatenate(
            [jnp.where(mask, high[run : run + 1, :], 0.0), jnp.where(mask, low[run : run + 1, :], 0.0)], axis=0
        ).astype(BF16)
        total = total + lax.dot_general(
            rows, cells[run], (((1,), (1,)), ((), ())), preferred_element_type=F32
        )
    plain[7] = jnp.where(cover > 0.5, total[0:128] + total[128:256], plain[7])

    @pl.when(shell < SHELLS - 1)
    def _():
        rim_up().wait_send()

    @pl.when(shell > 0)
    def _():
        rim_down().wait_send()


def hand_over(state, temp, new_state, thread_temp, sem):
    copies = [
        pltpu.make_async_copy(state, new_state, sem.at[0]),
        pltpu.make_async_copy(temp, thread_temp, sem.at[1]),
    ]
    for copy in copies:
        copy.start()
    for copy in copies:
        copy.wait()


def on_device(
    plasma_state, jacobian, send_list, recv_map, visit_point, visit_cell, conductance, lengths
):
    fields, blocks, cells = plasma_state.shape
    shape = jax.ShapeDtypeStruct
    vmem = pl.BlockSpec(memory_space=pltpu.VMEM)
    anywhere = pl.BlockSpec(memory_space=pl.ANY)
    dma = lambda *dims: pltpu.SemaphoreType.DMA(dims)
    buffer = lambda *dims: pltpu.VMEM(dims, F32)
    new_state, thread_temp = pl.pallas_call(
        whole_kernel,
        in_specs=[pl.BlockSpec(memory_space=pltpu.HBM)] * 8,
        out_specs=[vmem, vmem],
        out_shape=[pltpu.VMEM((fields, blocks, cells), F32), pltpu.VMEM((8, 512), F32)],
        scratch_shapes=[
            buffer(3, fields, fields, blocks),
            pltpu.VMEM(send_list.shape, jnp.int32),
            pltpu.VMEM((16, 128), jnp.int32),
            pltpu.VMEM((32, 128), jnp.int32),
            pltpu.VMEM((32, 128), jnp.int32),
            pltpu.VMEM((2, 128), jnp.int32),
            buffer(fields, 10, 80, 128),
            buffer(fields, 64, 128),
            buffer(fields, 64, 128),
            pltpu.VMEM((1280, 512), BF16),
            buffer(256, 128),
            pltpu.VMEM((1, 2432), jnp.int32),
            pltpu.VMEM((PEERS, 128), jnp.int32),
            pltpu.VMEM((PEERS, 128), jnp.int32),
            pltpu.VMEM((PEERS, 128), jnp.int32),
            buffer(PEERS, 128),
            pltpu.VMEM((1, 2048), jnp.int32),
            buffer(PEERS, 128, 128),
            buffer(PEERS, 128, 128),
            buffer(PEERS, 8, 128),
            buffer(8, 128),
            buffer(8, 128),
            buffer(8, 8, 128),
            buffer(SHELLS, 8, 128),
            buffer(272, 2048),
            buffer(4, fields, 8, 8, 128),
            buffer(fields, 8, 64, 128),
            buffer(3, 128),
            pltpu.VMEM((8, 512, 512), BF16),
            pltpu.VMEM((8, 128, 2048), BF16),
            pltpu.VMEM((8, 8, 2048), jnp.int32),
            buffer(8, 512),
            buffer(PEERS, 8, 128),
            buffer(PEERS, 8, 128),
            buffer(PEERS, 8, 128),
            buffer(PEERS, 8, 128),
            dma(8), dma(2), dma(2), dma(SHELLS), dma(SHELLS), dma(8), dma(8), dma(PEERS), dma(PEERS),
            dma(PEERS), dma(PEERS), dma(PEERS), dma(PEERS), dma(7),
        ],
        compiler_params=pltpu.CompilerParams(
            vmem_limit_bytes=VMEM_BYTES, collective_id=1, has_side_effects=True
        ),
        name="mhd_step",
    )(
        plasma_state, jacobian, send_list, recv_map.reshape(-1, 128), visit_point.reshape(-1, 128), visit_cell.reshape(-1, 128),
        conductance, lengths.reshape(-1, 128),
    )
    return pl.pallas_call(
        hand_over,
        in_specs=[vmem, vmem],
        out_specs=[anywhere, anywhere],
        out_shape=[shape((fields, blocks, cells), F32), shape((8, 512), F32)],
        scratch_shapes=[dma(2)],
        compiler_params=pltpu.CompilerParams(vmem_limit_bytes=4 * 1024 * 1024),
        name="hand_over",
    )(new_state, thread_temp)


def solution(mesh):
    in_specs = (
        P(None, ("shell", "blk"), None),
        P(None, None, None, ("shell", "blk")),
        P(None, ("shell", "blk")),
        P(("shell", "blk")),
        P(("shell", "blk")),
        P(("shell", "blk")),
        P("shell", None),
        P("shell"),
    )
    out_specs = (P(None, ("shell", "blk"), None), P(("shell", "blk"), None))
    return jax.shard_map(
        on_device, mesh=mesh, in_specs=in_specs, out_specs=out_specs, check_vma=False
    )
```
